256 devices in a mesh: gx: 16 (over z, core), gy: 16 (over x, y).
Axes of the slice: x: 4, y: 4, z: 8, core: 2. Of those that a mesh axis runs over, the one named last changes fastest.
Arguments:
- velocity: float32 [3, 2, 5, 5, 5, 16, 16, 256], P(None, None, None, None, None, 'gx', 'gy'), may hold values from -6 to 6
- convecting: float32 [3, 2, 5, 5, 5, 16, 16, 256], P(None, None, None, None, None, 'gx', 'gy'), may hold values from -6 to 6
- donor_element: int32 [25600], P(('gx', 'gy')), may hold values from 0 to 511
- coords: float32 [3, 25600], P(None, ('gx', 'gy')), may hold values from -1 to 1
- dest_rank: int32 [25600], P(('gx', 'gy')), may hold values from 0 to 255, as said below
- target: int32 [25600], P(('gx', 'gy')), may hold values from 0 to 99, as said below
Outputs:
- advected: float32 [3, 2, 5, 5, 5, 16, 16, 256], P(None, None, None, None, None, 'gx', 'gy')
The draws below stay inside these ranges and needn't reach their ends.
Inputs may be any that keep to these rules, and one draw needn't show every extreme that they name: Every interface point of every device is named by exactly one query, through dest_rank and target together. `dest_rank`: the queries held by one device name each device at most 1 times, and some device exactly that often.
All inputs are finite; a program needn't handle non-finite values.
Results may differ from the reference program's by a relative error of at most 0.0001.
Values sent between devices are 32-bit elements; how exact they have to be, the bound alone decides.
No kernel may reach another device: no remote copies, remote signals or barrier semaphores. Data moves between devices by JAX's collectives and lax.ppermute only.
A program may use at most 64 MiB of HBM per device.

```python
import math
from functools import partial
import jax
import jax.numpy as jnp
import numpy as np
from jax import lax

NP = 5
MESHES = 2
EXD = 1
EYD = 1
EZ = 256
ELEM_DEV = 512
NXE = 16
NYE = 16
RECV_DEV = 100
QUERIES = 25600
N_GX = 16
N_GY = 16


def route_tables(key):
    devices = N_GX * N_GY
    groups = RECV_DEV
    perm_keys = jax.random.split(key, 4)
    device_perm = jax.random.permutation(perm_keys[0], devices)
    rank_perm = jax.random.permutation(perm_keys[1], devices)
    device_inv = jnp.argsort(device_perm)
    rank_inv = jnp.argsort(rank_perm)
    donors = jnp.arange(devices)[:, None]
    group_ids = jnp.arange(groups)[None, :]
    receivers = rank_inv[(device_inv[donors] - group_ids) % devices]
    point_perm = jax.vmap(lambda subkey: jax.random.permutation(subkey, groups))(jax.random.split(perm_keys[2], devices))
    targets = point_perm[receivers, jnp.broadcast_to(group_ids, receivers.shape)]
    shuffle = jax.vmap(lambda subkey: jax.random.permutation(subkey, groups))(jax.random.split(perm_keys[3], devices))
    receivers = jnp.take_along_axis(receivers, shuffle, axis=1)
    targets = jnp.take_along_axis(targets, shuffle, axis=1)
    return (receivers.reshape(-1).astype(jnp.int32), targets.reshape(-1).astype(jnp.int32))


def draw_dest_rank(key, part):
    tables = route_tables(key)
    return tables[0]


def draw_target(key, part):
    tables = route_tables(key)
    return tables[1]


def set_ends(drawn, rng, least, top_value):
    index_at = [jax.random.randint(jax.random.fold_in(rng, axis), (), 0, length) for axis, length in enumerate(drawn.shape)]
    longest = drawn.shape.index(max(drawn.shape))
    neighbour = index_at[:longest] + [(index_at[longest] + 1) % drawn.shape[longest]] + index_at[longest + 1:]
    return drawn.at[tuple(index_at)].set(least).at[tuple(neighbour)].set(top_value)


def level_of(own_key, shape, cuts, low, top_value):
    def one(position, shards_of):
        heights = jax.random.uniform(jax.random.fold_in(jax.random.fold_in(own_key, 6), position), (shards_of,), jnp.float32, low / len(cuts), top_value / len(cuts))
        return jnp.repeat(jnp.exp(heights), shape[position] // shards_of).reshape((-1,) + (1,) * (len(shape) - position - 1))

    loudness = one(*cuts[0])
    for cut in cuts[1:]:
        loudness = loudness * one(*cut)
    return loudness


def noise(rng, shape, scale, most, cuts=(), kind=jnp.bfloat16):
    drawn = jax.random.normal(rng, shape, jnp.float32) * scale
    if len(cuts) > 0:
        drawn = level_of(rng, shape, cuts, -0.22, 0.18) * drawn
    return jnp.clip(drawn, min=-most, max=most).astype(kind)


def setup_inputs(seed: int = 0) -> dict:
    arg_keys = jax.random.split(jax.random.key(seed), 7)
    return {
        "velocity": noise(arg_keys[0], (3, MESHES, NP, NP, NP, NXE, NYE, EZ), 1.0, 6.0, ((5, 16), (6, 16)), jnp.float32),
        "convecting": noise(arg_keys[1], (3, MESHES, NP, NP, NP, NXE, NYE, EZ), 1.0, 6.0, ((5, 16), (6, 16)), jnp.float32),
        "donor_element": set_ends(jax.random.randint(arg_keys[2], (QUERIES,), 0, ELEM_DEV), jax.random.fold_in(arg_keys[2], 1), 0, ELEM_DEV - 1).astype(jnp.int32),
        "coords": jnp.clip(jax.random.uniform(arg_keys[3], (3, QUERIES), jnp.float32, -1.0, 1.0) * level_of(arg_keys[3], (3, QUERIES), ((1, 256),), -0.4, 0.0), -1.0, 1.0),
        "dest_rank": draw_dest_rank(jax.random.fold_in(arg_keys[6], 71), 0),
        "target": draw_target(jax.random.fold_in(arg_keys[6], 71), 0),
    }


time_step = 0.04

def gll_tables():
    root_value = math.sqrt(3.0 / 7.0)
    gll_nodes = [-1.0, -root_value, 0.0, root_value, 1.0]
    quad_weights = [0.1, 49.0 / 90.0, 32.0 / 45.0, 49.0 / 90.0, 0.1]
    bary_weights = []
    for index in range(5):
        product = 1.0
        for other_index in range(5):
            if other_index != index:
                product = product * (gll_nodes[index] - gll_nodes[other_index])
        bary_weights.append(1.0 / product)
    table = np.zeros((5, 5))
    for row_index in range(5):
        for col_index in range(5):
            if row_index != col_index:
                table[row_index, col_index] = bary_weights[col_index] / bary_weights[row_index] / (gll_nodes[row_index] - gll_nodes[col_index])
        table[row_index, row_index] = -np.sum(table[row_index])
    return (gll_nodes, quad_weights, table)

def lagrange(gll_nodes, points):
    basis = []
    for index in range(5):
        partial_value = jnp.ones_like(points)
        for other_index in range(5):
            if other_index != index:
                partial_value = partial_value * ((points - gll_nodes[other_index]) / (gll_nodes[index] - gll_nodes[other_index]))
        basis.append(partial_value)
    return jnp.stack(basis)

def face_sum(field, point_dim, neighbours):
    last_point = field.shape[point_dim] - 1
    lower_face = lax.index_in_dim(field, 0, point_dim, keepdims=False)
    upper_face = lax.index_in_dim(field, last_point, point_dim, keepdims=False)
    lower_next, upper_prev = neighbours(lower_face, upper_face)
    interior = lax.slice_in_dim(field, 1, last_point, axis=point_dim)
    return jnp.concatenate([jnp.expand_dims(lower_face + upper_prev, point_dim), interior, jnp.expand_dims(upper_face + lower_next, point_dim)], axis=point_dim)

def local_neighbours(lower_face, upper_face, face_dim):
    count_here = lower_face.shape[face_dim]
    zero_face = jnp.zeros_like(lax.slice_in_dim(lower_face, 0, 1, axis=face_dim))
    lower_next = jnp.concatenate([lax.slice_in_dim(lower_face, 1, count_here, axis=face_dim), zero_face], axis=face_dim)
    upper_prev = jnp.concatenate([zero_face, lax.slice_in_dim(upper_face, 0, count_here - 1, axis=face_dim)], axis=face_dim)
    return (lower_next, upper_prev)

def direct_sum(field):
    field = face_sum(field, 2, partial(local_neighbours, face_dim=4))
    field = face_sum(field, 3, partial(local_neighbours, face_dim=5))
    return face_sum(field, 4, partial(local_neighbours, face_dim=6))

def tendency(field, convecting, derivative, quad_mass, mass_sum, rhs_mask):
    highest = lax.Precision.HIGHEST
    grad_r = jnp.einsum('ai,cmijkxyz->cmajkxyz', derivative, field, precision=highest)
    grad_s = jnp.einsum('aj,cmijkxyz->cmiakxyz', derivative, field, precision=highest)
    grad_t = jnp.einsum('ak,cmijkxyz->cmijaxyz', derivative, field, precision=highest)
    advect = convecting[0] * grad_r + convecting[1] * grad_s + convecting[2] * grad_t
    weighted = -(quad_mass * advect)
    return direct_sum(weighted) / mass_sum * rhs_mask

def reference(velocity, convecting, donor_element, coords, dest_rank, target):
    gll_nodes, quad_weights, table = gll_tables()
    derivative = jnp.asarray(table, jnp.float32)
    weight_line = jnp.asarray(np.array(quad_weights), jnp.float32)
    quad_mass = (weight_line[:, None, None] * weight_line[None, :, None] * weight_line[None, None, :]).reshape(5, 5, 5, 1, 1, 1)
    query_index = jnp.arange(QUERIES, dtype=jnp.int32)
    device_rank = query_index // RECV_DEV
    device_x = device_rank // N_GY
    device_y = device_rank % N_GY
    mesh_id = donor_element // (EXD * EYD * EZ)
    elem_x = donor_element // (EYD * EZ) % EXD
    elem_y = donor_element // EZ % EYD
    elem_z = donor_element % EZ
    column_id = (((mesh_id * NXE + device_x * EXD + elem_x) * NYE + device_y * EYD + elem_y) * EZ + elem_z).astype(jnp.int32)
    columns = jnp.transpose(velocity, (0, 2, 3, 4, 1, 5, 6, 7)).reshape(3 * NP * NP * NP, -1)
    picked = jnp.take(columns, column_id, axis=1).reshape(3, NP, NP, NP, QUERIES)
    basis_r = lagrange(gll_nodes, coords[0])
    basis_s = lagrange(gll_nodes, coords[1])
    basis_t = lagrange(gll_nodes, coords[2])
    values = jnp.einsum('cijkq,iq,jq,kq->cq', picked, basis_r, basis_s, basis_t, precision=lax.Precision.HIGHEST)
    slot_id = (dest_rank * RECV_DEV + target).astype(jnp.int32)
    interface = jnp.zeros((3, QUERIES), jnp.float32).at[:, slot_id].set(values)
    interface = interface.reshape(3, N_GX, N_GY, MESHES, 2, NP, NP, EXD, EYD)
    interface = jnp.transpose(interface, (0, 3, 4, 5, 6, 1, 7, 2, 8)).reshape(3, MESHES, 2, NP, NP, NXE, NYE)
    initial = velocity.at[:, :, :, :, 0, :, :, 0].set(interface[:, :, 0])
    initial = initial.at[:, :, :, :, NP - 1, :, :, EZ - 1].set(interface[:, :, 1])
    mass_sum = direct_sum(jnp.broadcast_to(quad_mass, (1, MESHES, NP, NP, NP, NXE, NYE, EZ)).astype(jnp.float32))
    point_k = jnp.arange(NP)[:, None]
    elem_k = jnp.arange(EZ)[None, :]
    pinned = (point_k == 0) & (elem_k == 0) | (point_k == NP - 1) & (elem_k == EZ - 1)
    rhs_mask = jnp.where(pinned, 0.0, 1.0).astype(jnp.float32).reshape(NP, 1, 1, EZ)

    def slope(field):
        return tendency(field, convecting, derivative, quad_mass, mass_sum, rhs_mask)
    slope_one = slope(initial)
    slope_two = slope(initial + 0.5 * time_step * slope_one)
    slope_three = slope(initial + 0.5 * time_step * slope_two)
    slope_four = slope(initial + time_step * slope_three)
    return initial + time_step / 6.0 * (slope_one + 2.0 * slope_two + 2.0 * slope_three + slope_four)
```

```python
import functools
import math

import jax
import jax.numpy as jnp
import numpy as np
from jax import lax
from jax.experimental import pallas as pl
from jax.experimental.pallas import tpu as pltpu
from jax.sharding import PartitionSpec as P

time_step = 0.04
NP = 5
PTS = NP * NP * NP
ROWS = 6
EZ = 256
SLOT = 8
f32 = jnp.float32


def gll_tables():
    root_value = math.sqrt(3.0 / 7.0)
    nodes = [-1.0, -root_value, 0.0, root_value, 1.0]
    bary = []
    for i in range(NP):
        product = 1.0
        for j in range(NP):
            if j != i:
                product = product * (nodes[i] - nodes[j])
        bary.append(1.0 / product)
    table = np.zeros((NP, NP))
    for a in range(NP):
        for i in range(NP):
            if a != i:
                table[a, i] = bary[i] / bary[a] / (nodes[a] - nodes[i])
        table[a, a] = -np.sum(table[a])
    return nodes, table


NODES, D = gll_tables()


def pt(i, j, k):
    return (i * NP + j) * NP + k


def line_derivative(u):
    d0, d1 = u[0] - u[4], u[1] - u[3]
    s0, s1 = u[0] + u[4], u[1] + u[3]
    out = [None] * NP
    out[2] = d0 * float(D[2, 0]) + d1 * float(D[2, 1])
    for a in (0, 1):
        odd = d0 * float((D[a, 0] - D[a, 4]) / 2) + d1 * float((D[a, 1] - D[a, 3]) / 2)
        even = (
            s0 * float((D[a, 0] + D[a, 4]) / 2)
            + s1 * float((D[a, 1] + D[a, 3]) / 2)
            + u[2] * float(D[a, 2])
        )
        out[a] = odd + even
        out[4 - a] = odd - even
    return out


def end_derivatives(u):
    d0, d1 = u[0] - u[4], u[1] - u[3]
    s0, s1 = u[0] + u[4], u[1] + u[3]
    odd = d0 * float((D[0, 0] - D[0, 4]) / 2) + d1 * float((D[0, 1] - D[0, 3]) / 2)
    even = (
        s0 * float((D[0, 0] + D[0, 4]) / 2)
        + s1 * float((D[0, 1] + D[0, 3]) / 2)
        + u[2] * float(D[0, 2])
    )
    return odd + even, odd - even


def lane_index():
    return lax.broadcasted_iota(jnp.int32, (ROWS, EZ), 1)


def row_index():
    return lax.broadcasted_iota(jnp.int32, (ROWS, EZ), 0)


def place():
    a, b = lax.axis_index("gx"), lax.axis_index("gy")
    n, m = lax.axis_size("gx"), lax.axis_size("gy")
    ea, eb = a % 2 == 0, b % 2 == 0
    ia, ja = jnp.where(ea, 4, 0), jnp.where(eb, 4, 0)
    sx = jnp.where((a == 0) | (a == n - 1), 0.0, 1.0).astype(f32)
    sy = jnp.where((b == 0) | (b == m - 1), 0.0, 1.0).astype(f32)
    return a, b, n, m, ea, eb, ia, ja, sx, sy


def widen(two, odd_row):
    return jnp.where(odd_row, two[1:2], two[0:1])


def z_sum(ref, ij):
    low, high = ref[ij * NP], ref[ij * NP + 4]
    ref[ij * NP] = low + pltpu.roll(high, 1, 1)
    ref[ij * NP + 4] = high + pltpu.roll(low, EZ - 1, 1)


def first_kernel(vel, conv, u8, c0, c1, c2, w, xa, xb):
    a, b, n, m, ea, eb, ia, ja, sx, sy = place()
    lane, odd_row = lane_index(), row_index() % 2 == 1
    hx = {0: jnp.where(a > 0, 0.5, 1.0), 4: jnp.where(a < n - 1, 0.5, 1.0)}
    hy = {0: jnp.where(b > 0, 0.5, 1.0), 4: jnp.where(b < m - 1, 0.5, 1.0)}
    one = jnp.full((ROWS, EZ), -1.0, f32)
    hz = {
        0: jnp.where(lane == 0, 0.0, -0.5).astype(f32),
        4: jnp.where(lane == EZ - 1, 0.0, -0.5).astype(f32),
    }
    for i in range(NP):
        for j in range(NP):
            side = hx.get(i, 1.0) * hy.get(j, 1.0)
            for k in range(NP):
                p = pt(i, j, k)
                scale = hz.get(k, one)
                if i in hx or j in hy:
                    scale = scale * side.astype(f32)
                cc = conv[p] * scale
                c0[p] = widen(cc[0:2], odd_row)
                c1[p] = widen(cc[2:4], odd_row)
                c2[p] = widen(cc[4:6], odd_row)
                u8[p, 0:ROWS] = vel[p]
    for j in range(NP):
        for k in range(NP):
            g = line_derivative([vel[pt(i, j, k)] for i in range(NP)])
            for i in range(NP):
                w[pt(i, j, k)] = c0[pt(i, j, k)] * g[i]
    for i in range(NP):
        for k in range(NP):
            g = line_derivative([vel[pt(i, j, k)] for j in range(NP)])
            for j in range(NP):
                w[pt(i, j, k)] += c1[pt(i, j, k)] * g[j]
    for i in range(NP):
        for j in range(NP):
            u = [vel[pt(i, j, k)] for k in range(NP)]
            u[0] = jnp.where(lane == 0, 0.0, u[0])
            u[4] = jnp.where(lane == EZ - 1, 0.0, u[4])
            g = line_derivative(u)
            for k in range(NP):
                w[pt(i, j, k)] += c2[pt(i, j, k)] * g[k]
    for jk in range(NP * NP):
        pa, pb = ia * 25 + jk, (4 - ia) * 25 + jk
        xa[jk * 10 : jk * 10 + 6] = w[pa]
        xa[jk * 10 + 6 : jk * 10 + 8] = c1[pa, 0:2]
        xa[jk * 10 + 8 : jk * 10 + 10] = c2[pa, 0:2]
        xb[jk * 10 : jk * 10 + 6] = w[pb] * sx
        xb[jk * 10 + 6 : jk * 10 + 8] = c1[pb, 0:2] * sx
        xb[jk * 10 + 8 : jk * 10 + 10] = c2[pb, 0:2] * sx


def second_kernel(w, c0, c2, xa, xb, ya, yb):
    a, b, n, m, ea, eb, ia, ja, sx, sy = place()

    def edge(j_even, k, lo, hi, low_side):
        def at(j):
            r = (j * NP + k) * 10
            from_a, from_b = xa[r + lo : r + hi], xb[r + lo : r + hi]
            return jnp.where(ea, from_b, from_a) if low_side else jnp.where(ea, from_a, from_b)

        return jnp.where(j_even, at(4), at(0))

    for dst, jf, j_even, scale in ((ya, ja, eb, None), (yb, 4 - ja, jnp.logical_not(eb), sy)):
        put = (lambda x: x) if scale is None else (lambda x: x * scale)
        for i in range(NP):
            for k in range(NP):
                p = i * 25 + jf * NP + k
                r = (i * NP + k) * 10
                face = w[p]
                if i in (0, 4):
                    face = face + edge(j_even, k, 0, 6, i == 0)
                dst[r : r + 6] = put(face)
                dst[r + 6 : r + 8] = put(c0[p, 0:2])
                dst[r + 8 : r + 10] = put(c2[p, 0:2])
        for k in range(NP):
            for s, low_side in ((0, True), (1, False)):
                r = 250 + (s * NP + k) * 2
                dst[r : r + 2] = put(edge(j_even, k, 8, 10, low_side))


def query_kernel(u8, donor, coords, dest, target, table):
    queries = donor.shape[1]
    devices = table.shape[0]
    n, m = lax.axis_size("gx"), lax.axis_size("gy")
    lane_elem = donor[...] & (EZ - 1)
    hot = (
        lax.broadcasted_iota(jnp.int32, (EZ, queries), 0) == jnp.broadcast_to(lane_elem, (EZ, queries))
    ).astype(f32)
    grid = jnp.dot(
        u8[...].reshape(PTS * 8, EZ),
        hot,
        precision=lax.Precision.HIGHEST,
        preferred_element_type=f32,
    ).reshape(PTS, 8, queries)
    basis = []
    for d in range(3):
        x = coords[d : d + 1]
        line = []
        for i in range(NP):
            v = jnp.ones_like(x)
            for j in range(NP):
                if j != i:
                    v = v * ((x - NODES[j]) * (1.0 / (NODES[i] - NODES[j])))
            line.append(v)
        basis.append(line)
    total = jnp.zeros((8, queries), f32)
    for i in range(NP):
        for j in range(NP):
            part = grid[pt(i, j, 0)] * basis[2][0]
            for k in range(1, NP):
                part = part + grid[pt(i, j, k)] * basis[2][k]
            total = total + part * (basis[0][i] * basis[1][j])
    low = donor[...] < EZ
    rows = [jnp.where(low, total[2 * c : 2 * c + 1], total[2 * c + 1 : 2 * c + 2]) for c in range(3)]
    rows.append((target[...] + 1).astype(f32))
    row = lax.broadcasted_iota(jnp.int32, (8, queries), 0)
    packed = jnp.zeros((8, queries), f32)
    for r, x in enumerate(rows):
        packed = jnp.where(row == r, jnp.broadcast_to(x, (8, queries)), packed)
    goes = (
        lax.broadcasted_iota(jnp.int32, (devices, queries), 0)
        == jnp.broadcast_to(dest[...], (devices, queries))
    ).astype(f32)
    mine = lax.dot_general(
        packed,
        goes,
        (((1,), (1,)), ((), ())),
        precision=lax.Precision.HIGHEST,
        preferred_element_type=f32,
    )
    device = lax.broadcasted_iota(jnp.int32, (8, devices), 1)
    da, db = device // m, device % m

    def partner(x, pos, last, stride, first):
        even = pos % 2 == 0
        ahead, behind = pltpu.roll(x, devices - stride, 1), pltpu.roll(x, stride, 1)
        if first:
            return jnp.where(even, ahead, behind)
        return jnp.where((pos == 0) | (pos == last), 0.0, jnp.where(even, behind, ahead))

    x_a, x_b = partner(mine, da, n - 1, m, True), partner(mine, da, n - 1, m, False)
    slots = [mine, x_a, x_b]
    for first in (True, False):
        slots += [partner(s, db, m - 1, 1, first) for s in (mine, x_a, x_b)]
    slots.append(jnp.zeros((128 - SLOT * 9, devices), f32))
    table[...] = jnp.concatenate(slots, axis=0).T


def third_kernel(w_in, c0_in, c1_in, c2_in, u8, xa, xb, ya, yb, table, v, c0, c1, c2, acc, oxa, oxb, oya, oyb, z):
    a, b, n, m, ea, eb, ia, ja, sx, sy = place()
    del w_in, c0_in, c1_in, c2_in
    lane, row = lane_index(), row_index()
    odd_row = row % 2 == 1
    got = table[...].T
    base = (row % 2) * 50 + 1
    slope = [
        jnp.where(lane < EZ // 2, float(D[k, 0]), float(D[k, 4])).astype(f32) for k in range(NP)
    ]

    def values(slot, points):
        r = slot * SLOT
        mine = jnp.where(row < 2, got[r : r + 1], jnp.where(row < 4, got[r + 1 : r + 2], got[r + 2 : r + 3]))
        key = got[r + 3 : r + 4] - base.astype(f32)
        for where, ij in points:
            ends = []
            for side in range(2):
                hit = key == jnp.asarray(side * 25 + ij).astype(f32)
                ends.append(jnp.sum(jnp.where(hit, mine, 0.0), axis=1, keepdims=True))
            z[where] = jnp.where(lane == 0, ends[0], jnp.where(lane == EZ - 1, ends[1], 0.0))

    ib, jb = 4 - ia, 4 - ja
    values(0, [(ij, ij) for ij in range(25)])
    values(1, [(25 + j, ib * NP + j) for j in range(NP)])
    values(2, [(30 + j, ia * NP + j) for j in range(NP)])
    values(3, [(35 + i, i * NP + jb) for i in range(NP)])
    values(6, [(40 + i, i * NP + ja) for i in range(NP)])
    values(4, [(45, ib * NP + jb)])
    values(5, [(46, ia * NP + jb)])
    values(7, [(47, ib * NP + ja)])
    values(8, [(48, ia * NP + ja)])

    for ij in range(25):
        zz = z[ij]
        for k in range(NP):
            p = ij * NP + k
            v[p] += c2[p] * (zz * slope[k])
            u = u8[p, 0:ROWS]
            if k == 0:
                u = jnp.where(lane == 0, zz, u)
            if k == 4:
                u = jnp.where(lane == EZ - 1, zz, u)
            acc[p] = u
    for src, face, z0 in ((xa, ia, 25), (xb, ib, 30)):
        for j in range(NP):
            zz = z[z0 + j]
            for k in range(NP):
                r = (j * NP + k) * 10
                p = face * 25 + j * NP + k
                extra = widen(src[r + 8 : r + 10], odd_row)
                v[p] += src[r : r + 6] + extra * (zz * slope[k])
                c1[p] += widen(src[r + 6 : r + 8], odd_row)
                c2[p] += extra
    for src, face, z0, zd in ((ya, ja, 35, 45), (yb, jb, 40, 47)):
        for i in range(NP):
            zz = z[z0 + i]
            for k in range(NP):
                r = (i * NP + k) * 10
                p = i * 25 + face * NP + k
                extra = widen(src[r + 8 : r + 10], odd_row)
                add = src[r : r + 6] + extra * (zz * slope[k])
                if i in (0, 4):
                    r = 250 + ((i // 4) * NP + k) * 2
                    far = widen(src[r : r + 2], odd_row)
                    through_a = ea if i == 4 else jnp.logical_not(ea)
                    zfar = jnp.where(through_a, z[zd], z[zd + 1])
                    add = add + far * (zfar * slope[k])
                    extra = extra + far
                v[p] += add
                c0[p] += widen(src[(i * NP + k) * 10 + 6 : (i * NP + k) * 10 + 8], odd_row)
                c2[p] += extra
    for ij in range(25):
        z_sum(v, ij)
        z_sum(c0, ij)
        z_sum(c1, ij)
    messages(v, c0, c1, oxa, oxb, oya, oyb)


def messages(v, c0, c1, oxa, oxb, oya, oyb):
    a, b, n, m, ea, eb, ia, ja, sx, sy = place()
    for i in range(NP):
        for k in range(NP):
            low, high = end_derivatives([v[pt(i, j, k)] for j in range(NP)])
            low, high = low * c1[pt(i, 0, k)], high * c1[pt(i, 4, k)]
            r = (i * NP + k) * 6
            oya[r : r + 6] = jnp.where(eb, high, low)
            oyb[r : r + 6] = jnp.where(eb, low, high) * sy
    for j in range(NP):
        for k in range(NP):
            low, high = end_derivatives([v[pt(i, j, k)] for i in range(NP)])
            low, high = low * c0[pt(0, j, k)], high * c0[pt(4, j, k)]
            r = (j * NP + k) * 6
            oxa[r : r + 6] = jnp.where(ea, high, low)
            oxb[r : r + 6] = jnp.where(ea, low, high) * sx


def take_messages(v, xa, xb, ya, yb):
    a, b, n, m, ea, eb, ia, ja, sx, sy = place()
    for src, face in ((xa, ia), (xb, 4 - ia)):
        for jk in range(25):
            v[face * 25 + jk] += src[jk * 6 : jk * 6 + 6]
    for src, face in ((ya, ja), (yb, 4 - ja)):
        for i in range(NP):
            for k in range(NP):
                r = (i * NP + k) * 6
                v[i * 25 + face * NP + k] += src[r : r + 6]


def send_kernel(w_in, c0, c1, xa, xb, ya, yb, v, oxa, oxb, oya, oyb):
    del w_in
    take_messages(v, xa, xb, ya, yb)
    messages(v, c0, c1, oxa, oxb, oya, oyb)


def local_kernel(coef, v, c0, c1, c2, acc_in, acc, w):
    del acc_in
    for j in range(NP):
        for k in range(NP):
            u = [v[pt(i, j, k)] for i in range(NP)]
            g = line_derivative(u)
            for i in range(NP):
                p = pt(i, j, k)
                acc[p] += u[i] * coef
                w[p] = c0[p] * g[i]
    for i in range(NP):
        for k in range(NP):
            g = line_derivative([v[pt(i, j, k)] for j in range(NP)])
            for j in range(NP):
                w[pt(i, j, k)] += c1[pt(i, j, k)] * g[j]
    for i in range(NP):
        for j in range(NP):
            g = line_derivative([v[pt(i, j, k)] for k in range(NP)])
            t = [c2[pt(i, j, k)] * g[k] for k in range(NP)]
            t[0], t[4] = t[0] + pltpu.roll(t[4], 1, 1), t[4] + pltpu.roll(t[0], EZ - 1, 1)
            for k in range(NP):
                w[pt(i, j, k)] += t[k]


def last_kernel(coef, w_in, acc, xa, xb, ya, yb, v, out):
    del w_in
    take_messages(v, xa, xb, ya, yb)
    for p in range(PTS):
        out[p] = acc[p] + v[p] * coef


FIELD = (PTS, ROWS, EZ)


def call(kernel, outs, args, aliases=None, scratch=(), flops=0):
    moved = sum(4 * math.prod(x.shape) for x in args) + sum(4 * math.prod(s) for s in outs)
    return pl.pallas_call(
        kernel,
        out_shape=[jax.ShapeDtypeStruct(s, f32) for s in outs],
        in_specs=[pl.BlockSpec(memory_space=pltpu.VMEM)] * len(args),
        out_specs=[pl.BlockSpec(memory_space=pltpu.VMEM)] * len(outs),
        input_output_aliases=aliases or {},
        scratch_shapes=list(scratch),
        compiler_params=pltpu.CompilerParams(vmem_limit_bytes=24 * 1024 * 1024),
        cost_estimate=pl.CostEstimate(flops=flops, bytes_accessed=moved, transcendentals=0),
    )(*args)


def pairs(size, offset):
    route = []
    for low in range(offset, size, 2):
        high = (low + 1) % size
        route += [(low, high), (high, low)]
    return route


def swap(x, axis, offset):
    return lax.ppermute(x, axis, pairs(lax.axis_size(axis), offset))


def swap_all(xa, xb, ya, yb):
    return swap(xa, "gx", 0), swap(xb, "gx", 1), swap(ya, "gy", 0), swap(yb, "gy", 1)


def body(velocity, convecting, donor_element, coords, dest_rank, target):
    devices = lax.axis_size("gx") * lax.axis_size("gy")
    queries = dest_rank.shape[0]
    vel = jnp.transpose(velocity.reshape(ROWS, PTS, EZ), (1, 0, 2))
    conv = jnp.transpose(convecting.reshape(ROWS, PTS, EZ), (1, 0, 2))
    u8, c0, c1, c2, w, xa, xb = call(
        first_kernel, [(PTS, 8, EZ)] + [FIELD] * 4 + [(250, EZ)] * 2, [vel, conv]
    )
    xa, xb = swap(xa, "gx", 0), swap(xb, "gx", 1)
    (table,) = call(
        query_kernel,
        [(devices, 128)],
        [
            u8,
            donor_element.reshape(1, queries),
            coords,
            dest_rank.reshape(1, queries),
            target.reshape(1, queries),
        ],
    )
    ya, yb = call(second_kernel, [(270, EZ)] * 2, [w, c0, c2, xa, xb])
    table, ya, yb = lax.optimization_barrier((table, ya, yb))
    ya, yb = swap(ya, "gy", 0), swap(yb, "gy", 1)
    table = lax.all_to_all(table.reshape(devices, 1, 128), ("gx", "gy"), 0, 0).reshape(devices, 128)
    v, c0, c1, c2, acc, oxa, oxb, oya, oyb = call(
        third_kernel,
        [FIELD] * 5 + [(150, EZ)] * 4,
        [w, c0, c1, c2, u8, xa, xb, ya, yb, table],
        aliases={0: 0, 1: 1, 2: 2, 3: 3},
        scratch=[pltpu.VMEM((49, ROWS, EZ), f32)],
    )
    coef = 1.0
    for stage in range(1, 4):
        coef = coef * time_step / stage
        got = swap_all(oxa, oxb, oya, oyb)
        acc, w = call(
            functools.partial(local_kernel, coef),
            [FIELD] * 2,
            [v, c0, c1, c2, acc],
            aliases={4: 0},
            flops=10**7,
        )
        if stage < 3:
            v, oxa, oxb, oya, oyb = call(
                send_kernel, [FIELD] + [(150, EZ)] * 4, [w, c0, c1, *got], aliases={0: 0}
            )
    coef = coef * time_step / 4
    _, out = call(
        functools.partial(last_kernel, coef), [FIELD] * 2, [w, acc, *got], aliases={0: 0}
    )
    return jnp.transpose(out, (1, 0, 2)).reshape(velocity.shape)


def solution(mesh):
    field = P(None, None, None, None, None, "gx", "gy", None)
    return jax.shard_map(
        body,
        mesh=mesh,
        in_specs=(field, field, P(("gx", "gy")), P(None, ("gx", "gy")), P(("gx", "gy")), P(("gx", "gy"))),
        out_specs=field,
        check_vma=False,
    )
```

```python
import functools
import math

import jax
import jax.numpy as jnp
import numpy as np
from jax import lax
from jax.experimental import pallas as pl
from jax.experimental.pallas import tpu as pltpu
from jax.sharding import PartitionSpec as P

time_step = 0.04
NP = 5
PTS = NP * NP * NP
ROWS = 6
EZ = 256
SLOT = 8
f32 = jnp.float32


def gll_tables():
    root_value = math.sqrt(3.0 / 7.0)
    nodes = [-1.0, -root_value, 0.0, root_value, 1.0]
    bary = []
    for i in range(NP):
        product = 1.0
        for j in range(NP):
            if j != i:
                product = product * (nodes[i] - nodes[j])
        bary.append(1.0 / product)
    table = np.zeros((NP, NP))
    for a in range(NP):
        for i in range(NP):
            if a != i:
                table[a, i] = bary[i] / bary[a] / (nodes[a] - nodes[i])
        table[a, a] = -np.sum(table[a])
    return nodes, table


NODES, D = gll_tables()


def pt(i, j, k):
    return (i * NP + j) * NP + k


def line_derivative(u):
    d0, d1 = u[0] - u[4], u[1] - u[3]
    s0, s1 = u[0] + u[4], u[1] + u[3]
    out = [None] * NP
    out[2] = d0 * float(D[2, 0]) + d1 * float(D[2, 1])
    for a in (0, 1):
        odd = d0 * float((D[a, 0] - D[a, 4]) / 2) + d1 * float((D[a, 1] - D[a, 3]) / 2)
        even = (
            s0 * float((D[a, 0] + D[a, 4]) / 2)
            + s1 * float((D[a, 1] + D[a, 3]) / 2)
            + u[2] * float(D[a, 2])
        )
        out[a] = odd + even
        out[4 - a] = odd - even
    return out


def end_derivatives(u):
    d0, d1 = u[0] - u[4], u[1] - u[3]
    s0, s1 = u[0] + u[4], u[1] + u[3]
    odd = d0 * float((D[0, 0] - D[0, 4]) / 2) + d1 * float((D[0, 1] - D[0, 3]) / 2)
    even = (
        s0 * float((D[0, 0] + D[0, 4]) / 2)
        + s1 * float((D[0, 1] + D[0, 3]) / 2)
        + u[2] * float(D[0, 2])
    )
    return odd + even, odd - even


def lane_index():
    return lax.broadcasted_iota(jnp.int32, (ROWS, EZ), 1)


def row_index():
    return lax.broadcasted_iota(jnp.int32, (ROWS, EZ), 0)


def place():
    a, b = lax.axis_index("gx"), lax.axis_index("gy")
    n, m = lax.axis_size("gx"), lax.axis_size("gy")
    ea, eb = a % 2 == 0, b % 2 == 0
    ia, ja = jnp.where(ea, 4, 0), jnp.where(eb, 4, 0)
    sx = jnp.where((a == 0) | (a == n - 1), 0.0, 1.0).astype(f32)
    sy = jnp.where((b == 0) | (b == m - 1), 0.0, 1.0).astype(f32)
    return a, b, n, m, ea, eb, ia, ja, sx, sy


def widen(two, odd_row):
    return jnp.where(odd_row, two[1:2], two[0:1])


def z_sum(ref, ij):
    low, high = ref[ij * NP], ref[ij * NP + 4]
    ref[ij * NP] = low + pltpu.roll(high, 1, 1)
    ref[ij * NP + 4] = high + pltpu.roll(low, EZ - 1, 1)


def face_scale(lane, a, b, n, m):
    hx = {0: jnp.where(a > 0, 0.5, 1.0), 4: jnp.where(a < n - 1, 0.5, 1.0)}
    hy = {0: jnp.where(b > 0, 0.5, 1.0), 4: jnp.where(b < m - 1, 0.5, 1.0)}
    one = jnp.full((ROWS, EZ), -1.0, f32)
    hz = {
        0: jnp.where(lane == 0, 0.0, -0.5).astype(f32),
        4: jnp.where(lane == EZ - 1, 0.0, -0.5).astype(f32),
    }

    def scale(i, j, k):
        side = hx.get(i, 1.0) * hy.get(j, 1.0)
        out = hz.get(k, one)
        return out * side.astype(f32) if i in hx or j in hy else out

    return scale


def pinned_line(u, lane):
    u[0] = jnp.where(lane == 0, 0.0, u[0])
    u[4] = jnp.where(lane == EZ - 1, 0.0, u[4])
    return u


def row_copies(src, dst, sem, first, count):
    return [
        pltpu.make_async_copy(
            src.at[r, pl.ds(first, count), 0, :], dst.at[pl.ds(first, count), r, :], sem.at[r]
        )
        for r in range(ROWS)
    ]


def opening_kernel(vel, conv, u8, xa, xb, cbuf, sem):
    a, b, n, m, ea, eb, ia, ja, sx, sy = place()
    copies = row_copies(vel, u8, sem.at[0], 0, PTS)
    faces = row_copies(conv, cbuf, sem.at[1], 0, 25) + row_copies(conv, cbuf, sem.at[2], 100, 25)
    for c in copies + faces:
        c.start()
    lane, odd_row = lane_index(), row_index() % 2 == 1
    scale = face_scale(lane, a, b, n, m)
    for c in copies + faces:
        c.wait()
    done = {}
    for i in (0, 4):
        gs, gt = {}, {}
        for k in range(NP):
            line = line_derivative([u8[pt(i, j, k), 0:ROWS] for j in range(NP)])
            for j in range(NP):
                gs[j, k] = line[j]
        for j in range(NP):
            line = line_derivative(pinned_line([u8[pt(i, j, k), 0:ROWS] for k in range(NP)], lane))
            for k in range(NP):
                gt[j, k] = line[k]
        for j in range(NP):
            for k in range(NP):
                cc = cbuf[pt(i, j, k), 0:ROWS] * scale(i, j, k)
                ends = end_derivatives([u8[pt(q, j, k), 0:ROWS] for q in range(NP)])
                w = (
                    widen(cc[0:2], odd_row) * ends[i // 4]
                    + widen(cc[2:4], odd_row) * gs[j, k]
                    + widen(cc[4:6], odd_row) * gt[j, k]
                )
                r = (j * NP + k) * 10
                if i == 0:
                    xa[r : r + 6], xa[r + 6 : r + 10] = w, cc[2:6]
                else:
                    low, clow = xa[r : r + 6], xa[r + 6 : r + 10]
                    xa[r : r + 6] = jnp.where(ea, w, low)
                    xa[r + 6 : r + 10] = jnp.where(ea, cc[2:6], clow)
                    xb[r : r + 6] = jnp.where(ea, low, w) * sx
                    xb[r + 6 : r + 10] = jnp.where(ea, clow, cc[2:6]) * sx


def coefficients(u8, cbuf, c0, c1, c2, w):
    a, b, n, m, ea, eb, ia, ja, sx, sy = place()
    lane, odd_row = lane_index(), row_index() % 2 == 1
    scale = face_scale(lane, a, b, n, m)
    for i in range(NP):
        for j in range(NP):
            for k in range(NP):
                p = pt(i, j, k)
                cc = cbuf[p, 0:ROWS] * scale(i, j, k)
                c0[p] = widen(cc[0:2], odd_row)
                c1[p] = widen(cc[2:4], odd_row)
                c2[p] = widen(cc[4:6], odd_row)
    for j in range(NP):
        for k in range(NP):
            g = line_derivative([u8[pt(i, j, k), 0:ROWS] for i in range(NP)])
            for i in range(NP):
                w[pt(i, j, k)] = c0[pt(i, j, k)] * g[i]
    for i in range(NP):
        for k in range(NP):
            g = line_derivative([u8[pt(i, j, k), 0:ROWS] for j in range(NP)])
            for j in range(NP):
                w[pt(i, j, k)] += c1[pt(i, j, k)] * g[j]
    for i in range(NP):
        for j in range(NP):
            g = line_derivative(pinned_line([u8[pt(i, j, k), 0:ROWS] for k in range(NP)], lane))
            for k in range(NP):
                w[pt(i, j, k)] += c2[pt(i, j, k)] * g[k]


def query_kernel(u8, conv, donor, coords, dest, target, table, c0, c1, c2, w, cbuf, sem):
    copies = row_copies(conv, cbuf, sem, 0, PTS)
    for c in copies:
        c.start()
    make_table(u8, donor, coords, dest, target, table)
    for c in copies:
        c.wait()
    coefficients(u8, cbuf, c0, c1, c2, w)


def second_kernel(w, c0, c2, xa, xb, ya, yb):
    a, b, n, m, ea, eb, ia, ja, sx, sy = place()

    def edge(j_even, k, lo, hi, low_side):
        def at(j):
            r = (j * NP + k) * 10
            from_a, from_b = xa[r + lo : r + hi], xb[r + lo : r + hi]
            return jnp.where(ea, from_b, from_a) if low_side else jnp.where(ea, from_a, from_b)

        return jnp.where(j_even, at(4), at(0))

    for dst, jf, j_even, scale in ((ya, ja, eb, None), (yb, 4 - ja, jnp.logical_not(eb), sy)):
        put = (lambda x: x) if scale is None else (lambda x: x * scale)
        for i in range(NP):
            for k in range(NP):
                p = i * 25 + jf * NP + k
                r = (i * NP + k) * 10
                face = w[p]
                if i in (0, 4):
                    face = face + edge(j_even, k, 0, 6, i == 0)
                dst[r : r + 6] = put(face)
                dst[r + 6 : r + 8] = put(c0[p, 0:2])
                dst[r + 8 : r + 10] = put(c2[p, 0:2])
        for k in range(NP):
            for s, low_side in ((0, True), (1, False)):
                r = 250 + (s * NP + k) * 2
                dst[r : r + 2] = put(edge(j_even, k, 8, 10, low_side))


def make_table(u8, donor, coords, dest, target, table):
    queries = donor.shape[1]
    devices = table.shape[0]
    n, m = lax.axis_size("gx"), lax.axis_size("gy")
    lane_elem = donor[...] & (EZ - 1)
    hot = (
        lax.broadcasted_iota(jnp.int32, (EZ, queries), 0) == jnp.broadcast_to(lane_elem, (EZ, queries))
    ).astype(f32)
    grid = jnp.dot(
        u8[...].reshape(PTS * 8, EZ),
        hot,
        precision=lax.Precision.HIGHEST,
        preferred_element_type=f32,
    ).reshape(PTS, 8, queries)
    basis = []
    for d in range(3):
        x = coords[d : d + 1]
        line = []
        for i in range(NP):
            v = jnp.ones_like(x)
            for j in range(NP):
                if j != i:
                    v = v * ((x - NODES[j]) * (1.0 / (NODES[i] - NODES[j])))
            line.append(v)
        basis.append(line)
    total = jnp.zeros((8, queries), f32)
    for i in range(NP):
        for j in range(NP):
            part = grid[pt(i, j, 0)] * basis[2][0]
            for k in range(1, NP):
                part = part + grid[pt(i, j, k)] * basis[2][k]
            total = total + part * (basis[0][i] * basis[1][j])
    low = donor[...] < EZ
    rows = [jnp.where(low, total[2 * c : 2 * c + 1], total[2 * c + 1 : 2 * c + 2]) for c in range(3)]
    rows.append((target[...] + 1).astype(f32))
    row = lax.broadcasted_iota(jnp.int32, (8, queries), 0)
    packed = jnp.zeros((8, queries), f32)
    for r, x in enumerate(rows):
        packed = jnp.where(row == r, jnp.broadcast_to(x, (8, queries)), packed)
    goes = (
        lax.broadcasted_iota(jnp.int32, (devices, queries), 0)
        == jnp.broadcast_to(dest[...], (devices, queries))
    ).astype(f32)
    mine = lax.dot_general(
        packed,
        goes,
        (((1,), (1,)), ((), ())),
        precision=lax.Precision.HIGHEST,
        preferred_element_type=f32,
    )
    device = lax.broadcasted_iota(jnp.int32, (8, devices), 1)
    da, db = device // m, device % m

    def partner(x, pos, last, stride, first):
        even = pos % 2 == 0
        ahead, behind = pltpu.roll(x, devices - stride, 1), pltpu.roll(x, stride, 1)
        if first:
            return jnp.where(even, ahead, behind)
        return jnp.where((pos == 0) | (pos == last), 0.0, jnp.where(even, behind, ahead))

    x_a, x_b = partner(mine, da, n - 1, m, True), partner(mine, da, n - 1, m, False)
    slots = [mine, x_a, x_b]
    for first in (True, False):
        slots += [partner(s, db, m - 1, 1, first) for s in (mine, x_a, x_b)]
    slots.append(jnp.zeros((128 - SLOT * 9, devices), f32))
    table[...] = jnp.concatenate(slots, axis=0).T


def third_kernel(w_in, c0_in, c1_in, c2_in, u8, xa, xb, ya, yb, table, v, c0, c1, c2, acc, oya, oyb, z):
    a, b, n, m, ea, eb, ia, ja, sx, sy = place()
    del w_in, c0_in, c1_in, c2_in
    lane, row = lane_index(), row_index()
    odd_row = row % 2 == 1
    got = table[...].T
    base = (row % 2) * 50 + 1
    slope = [
        jnp.where(lane < EZ // 2, float(D[k, 0]), float(D[k, 4])).astype(f32) for k in range(NP)
    ]

    def values(slot, points):
        r = slot * SLOT
        mine = jnp.where(row < 2, got[r : r + 1], jnp.where(row < 4, got[r + 1 : r + 2], got[r + 2 : r + 3]))
        key = got[r + 3 : r + 4] - base.astype(f32)
        for where, ij in points:
            ends = []
            for side in range(2):
                hit = key == jnp.asarray(side * 25 + ij).astype(f32)
                ends.append(jnp.sum(jnp.where(hit, mine, 0.0), axis=1, keepdims=True))
            z[where] = jnp.where(lane == 0, ends[0], jnp.where(lane == EZ - 1, ends[1], 0.0))

    ib, jb = 4 - ia, 4 - ja
    values(0, [(ij, ij) for ij in range(25)])
    values(1, [(25 + j, ib * NP + j) for j in range(NP)])
    values(2, [(30 + j, ia * NP + j) for j in range(NP)])
    values(3, [(35 + i, i * NP + jb) for i in range(NP)])
    values(6, [(40 + i, i * NP + ja) for i in range(NP)])
    values(4, [(45, ib * NP + jb)])
    values(5, [(46, ia * NP + jb)])
    values(7, [(47, ib * NP + ja)])
    values(8, [(48, ia * NP + ja)])

    for ij in range(25):
        zz = z[ij]
        for k in range(NP):
            p = ij * NP + k
            v[p] += c2[p] * (zz * slope[k])
            u = u8[p, 0:ROWS]
            if k == 0:
                u = jnp.where(lane == 0, zz, u)
            if k == 4:
                u = jnp.where(lane == EZ - 1, zz, u)
            acc[p] = u
    for src, face, z0 in ((xa, ia, 25), (xb, ib, 30)):
        for j in range(NP):
            zz = z[z0 + j]
            for k in range(NP):
                r = (j * NP + k) * 10
                p = face * 25 + j * NP + k
                extra = widen(src[r + 8 : r + 10], odd_row)
                v[p] += src[r : r + 6] + extra * (zz * slope[k])
                c1[p] += widen(src[r + 6 : r + 8], odd_row)
                c2[p] += extra
    for src, face, z0, zd in ((ya, ja, 35, 45), (yb, jb, 40, 47)):
        for i in range(NP):
            zz = z[z0 + i]
            for k in range(NP):
                r = (i * NP + k) * 10
                p = i * 25 + face * NP + k
                extra = widen(src[r + 8 : r + 10], odd_row)
                add = src[r : r + 6] + extra * (zz * slope[k])
                if i in (0, 4):
                    r = 250 + ((i // 4) * NP + k) * 2
                    far = widen(src[r : r + 2], odd_row)
                    through_a = ea if i == 4 else jnp.logical_not(ea)
                    zfar = jnp.where(through_a, z[zd], z[zd + 1])
                    add = add + far * (zfar * slope[k])
                    extra = extra + far
                v[p] += add
                c0[p] += widen(src[(i * NP + k) * 10 + 6 : (i * NP + k) * 10 + 8], odd_row)
                c2[p] += extra
    for ij in range(25):
        z_sum(v, ij)
        z_sum(c0, ij)
        z_sum(c1, ij)
    second_messages(v, c1, oya, oyb)


def second_messages(v, c1, oya, oyb):
    a, b, n, m, ea, eb, ia, ja, sx, sy = place()
    for i in range(NP):
        for k in range(NP):
            low, high = end_derivatives([v[pt(i, j, k)] for j in range(NP)])
            low, high = low * c1[pt(i, 0, k)], high * c1[pt(i, 4, k)]
            r = (i * NP + k) * 6
            oya[r : r + 6] = jnp.where(eb, high, low)
            oyb[r : r + 6] = jnp.where(eb, low, high) * sy


def first_messages(v, c0, oxa, oxb):
    a, b, n, m, ea, eb, ia, ja, sx, sy = place()
    for j in range(NP):
        for k in range(NP):
            low, high = end_derivatives([v[pt(i, j, k)] for i in range(NP)])
            low, high = low * c0[pt(0, j, k)], high * c0[pt(4, j, k)]
            r = (j * NP + k) * 6
            oxa[r : r + 6] = jnp.where(ea, high, low)
            oxb[r : r + 6] = jnp.where(ea, low, high) * sx


def take_messages(v, xa, xb, ya, yb):
    a, b, n, m, ea, eb, ia, ja, sx, sy = place()
    for src, face in ((xa, ia), (xb, 4 - ia)):
        for jk in range(25):
            v[face * 25 + jk] += src[jk * 6 : jk * 6 + 6]
    for src, face in ((ya, ja), (yb, 4 - ja)):
        for i in range(NP):
            for k in range(NP):
                r = (i * NP + k) * 6
                v[i * 25 + face * NP + k] += src[r : r + 6]


def send_kernel(w_in, c1, xa, xb, ya, yb, v, oya, oyb):
    del w_in
    take_messages(v, xa, xb, ya, yb)
    second_messages(v, c1, oya, oyb)


def local_kernel(coef, v, c0, c1, c2, acc_in, acc, w):
    del acc_in
    for j in range(NP):
        for k in range(NP):
            u = [v[pt(i, j, k)] for i in range(NP)]
            g = line_derivative(u)
            for i in range(NP):
                p = pt(i, j, k)
                acc[p] += u[i] * coef
                w[p] = c0[p] * g[i]
    for i in range(NP):
        for k in range(NP):
            g = line_derivative([v[pt(i, j, k)] for j in range(NP)])
            for j in range(NP):
                w[pt(i, j, k)] += c1[pt(i, j, k)] * g[j]
    for i in range(NP):
        for j in range(NP):
            g = line_derivative([v[pt(i, j, k)] for k in range(NP)])
            t = [c2[pt(i, j, k)] * g[k] for k in range(NP)]
            t[0], t[4] = t[0] + pltpu.roll(t[4], 1, 1), t[4] + pltpu.roll(t[0], EZ - 1, 1)
            for k in range(NP):
                w[pt(i, j, k)] += t[k]


def last_kernel(coef, w_in, acc, xa, xb, ya, yb, v, out, obuf, sem):
    del w_in
    take_messages(v, xa, xb, ya, yb)
    started = []
    for i in range(NP):
        for p in range(i * 25, i * 25 + 25):
            obuf[p, 0:ROWS] = acc[p] + v[p] * coef
        for r in range(ROWS):
            rows = pl.ds(i * 25, 25)
            c = pltpu.make_async_copy(obuf.at[rows, r, :], out.at[r, rows, 0, :], sem.at[i, r])
            c.start()
            started.append(c)
    for c in started:
        c.wait()


FIELD = (PTS, ROWS, EZ)


RAW = (ROWS, PTS, 1, EZ)


def call(kernel, outs, args, aliases=None, scratch=(), flops=0):
    moved = sum(4 * math.prod(x.shape) for x in args) + sum(4 * math.prod(s) for s in outs)
    spec = lambda shape: pl.BlockSpec(memory_space=pl.ANY if shape == RAW else pltpu.VMEM)
    return pl.pallas_call(
        kernel,
        out_shape=[jax.ShapeDtypeStruct(s, f32) for s in outs],
        in_specs=[spec(x.shape) for x in args],
        out_specs=[spec(s) for s in outs],
        input_output_aliases=aliases or {},
        scratch_shapes=list(scratch),
        compiler_params=pltpu.CompilerParams(vmem_limit_bytes=24 * 1024 * 1024),
        cost_estimate=pl.CostEstimate(flops=flops, bytes_accessed=moved, transcendentals=0),
    )(*args)


def pairs(size, offset):
    route = []
    for low in range(offset, size, 2):
        high = (low + 1) % size
        route += [(low, high), (high, low)]
    return route


def swap(x, axis, offset):
    return lax.ppermute(x, axis, pairs(lax.axis_size(axis), offset))


def swap_all(xa, xb, ya, yb):
    return swap(xa, "gx", 0), swap(xb, "gx", 1), swap(ya, "gy", 0), swap(yb, "gy", 1)


def body(velocity, convecting, donor_element, coords, dest_rank, target):
    devices = lax.axis_size("gx") * lax.axis_size("gy")
    queries = dest_rank.shape[0]
    vel, conv = velocity.reshape(RAW), convecting.reshape(RAW)
    whole = pltpu.VMEM((PTS, 8, EZ), f32)
    u8, xa, xb = call(
        opening_kernel,
        [(PTS, 8, EZ)] + [(250, EZ)] * 2,
        [vel, conv],
        scratch=[whole, pltpu.SemaphoreType.DMA((3, ROWS))],
    )
    xa, xb = swap(xa, "gx", 0), swap(xb, "gx", 1)
    table, c0, c1, c2, w = call(
        query_kernel,
        [(devices, 128)] + [FIELD] * 4,
        [
            u8,
            conv,
            donor_element.reshape(1, queries),
            coords,
            dest_rank.reshape(1, queries),
            target.reshape(1, queries),
        ],
        scratch=[whole, pltpu.SemaphoreType.DMA((ROWS,))],
    )
    ya, yb = call(second_kernel, [(270, EZ)] * 2, [w, c0, c2, xa, xb])
    table, ya, yb = lax.optimization_barrier((table, ya, yb))
    ya, yb = swap(ya, "gy", 0), swap(yb, "gy", 1)
    table = lax.all_to_all(table.reshape(devices, 1, 128), ("gx", "gy"), 0, 0).reshape(devices, 128)
    v, c0, c1, c2, acc, ya, yb = call(
        third_kernel,
        [FIELD] * 5 + [(150, EZ)] * 2,
        [w, c0, c1, c2, u8, xa, xb, ya, yb, table],
        aliases={0: 0, 1: 1, 2: 2, 3: 3},
        scratch=[pltpu.VMEM((49, ROWS, EZ), f32)],
    )
    coef = 1.0
    for stage in range(1, 4):
        coef = coef * time_step / stage
        ya, yb = swap(ya, "gy", 0), swap(yb, "gy", 1)
        xa, xb = call(first_messages, [(150, EZ)] * 2, [v, c0])
        got = [swap(xa, "gx", 0), swap(xb, "gx", 1), ya, yb]
        acc, w = call(
            functools.partial(local_kernel, coef),
            [FIELD] * 2,
            [v, c0, c1, c2, acc],
            aliases={4: 0},
            flops=10**7,
        )
        if stage < 3:
            v, ya, yb = call(
                send_kernel, [FIELD] + [(150, EZ)] * 2, [w, c1, *got], aliases={0: 0}
            )
    coef = coef * time_step / 4
    _, out = call(
        functools.partial(last_kernel, coef),
        [FIELD, RAW],
        [w, acc, *got],
        aliases={0: 0},
        scratch=[whole, pltpu.SemaphoreType.DMA((NP, ROWS))],
    )
    return out.reshape(velocity.shape)


def solution(mesh):
    field = P(None, None, None, None, None, "gx", "gy", None)
    return jax.shard_map(
        body,
        mesh=mesh,
        in_specs=(field, field, P(("gx", "gy")), P(None, ("gx", "gy")), P(("gx", "gy")), P(("gx", "gy"))),
        out_specs=field,
        check_vma=False,
    )
```

```python
import functools
import math

import jax
import jax.numpy as jnp
import numpy as np
from jax import lax
from jax.experimental import pallas as pl
from jax.experimental.pallas import tpu as pltpu
from jax.sharding import PartitionSpec as P

time_step = 0.04
NP = 5
PTS = NP * NP * NP
ROWS = 6
EZ = 256
SLOT = 8
f32 = jnp.float32


def gll_tables():
    root_value = math.sqrt(3.0 / 7.0)
    nodes = [-1.0, -root_value, 0.0, root_value, 1.0]
    bary = []
    for i in range(NP):
        product = 1.0
        for j in range(NP):
            if j != i:
                product = product * (nodes[i] - nodes[j])
        bary.append(1.0 / product)
    table = np.zeros((NP, NP))
    for a in range(NP):
        for i in range(NP):
            if a != i:
                table[a, i] = bary[i] / bary[a] / (nodes[a] - nodes[i])
        table[a, a] = -np.sum(table[a])
    return nodes, table


NODES, D = gll_tables()


def pt(i, j, k):
    return (i * NP + j) * NP + k


def line_derivative(u):
    d0, d1 = u[0] - u[4], u[1] - u[3]
    s0, s1 = u[0] + u[4], u[1] + u[3]
    out = [None] * NP
    out[2] = d0 * float(D[2, 0]) + d1 * float(D[2, 1])
    for a in (0, 1):
        odd = d0 * float((D[a, 0] - D[a, 4]) / 2) + d1 * float((D[a, 1] - D[a, 3]) / 2)
        even = (
            s0 * float((D[a, 0] + D[a, 4]) / 2)
            + s1 * float((D[a, 1] + D[a, 3]) / 2)
            + u[2] * float(D[a, 2])
        )
        out[a] = odd + even
        out[4 - a] = odd - even
    return out


def end_derivatives(u):
    d0, d1 = u[0] - u[4], u[1] - u[3]
    s0, s1 = u[0] + u[4], u[1] + u[3]
    odd = d0 * float((D[0, 0] - D[0, 4]) / 2) + d1 * float((D[0, 1] - D[0, 3]) / 2)
    even = (
        s0 * float((D[0, 0] + D[0, 4]) / 2)
        + s1 * float((D[0, 1] + D[0, 3]) / 2)
        + u[2] * float(D[0, 2])
    )
    return odd + even, odd - even


def lane_index():
    return lax.broadcasted_iota(jnp.int32, (ROWS, EZ), 1)


def row_index():
    return lax.broadcasted_iota(jnp.int32, (ROWS, EZ), 0)


def place():
    a, b = lax.axis_index("gx"), lax.axis_index("gy")
    n, m = lax.axis_size("gx"), lax.axis_size("gy")
    ea, eb = a % 2 == 0, b % 2 == 0
    ia, ja = jnp.where(ea, 4, 0), jnp.where(eb, 4, 0)
    sx = jnp.where((a == 0) | (a == n - 1), 0.0, 1.0).astype(f32)
    sy = jnp.where((b == 0) | (b == m - 1), 0.0, 1.0).astype(f32)
    return a, b, n, m, ea, eb, ia, ja, sx, sy


def widen(two, odd_row):
    return jnp.where(odd_row, two[1:2], two[0:1])


def z_pair(line):
    line[0], line[4] = line[0] + pltpu.roll(line[4], 1, 1), line[4] + pltpu.roll(line[0], EZ - 1, 1)


def z_sum(ref, ij):
    line = [ref[ij * NP + k] for k in range(NP)]
    z_pair(line)
    ref[ij * NP], ref[ij * NP + 4] = line[0], line[4]


def face_scale(lane, a, b, n, m):
    hx = {0: jnp.where(a > 0, 0.5, 1.0), 4: jnp.where(a < n - 1, 0.5, 1.0)}
    hy = {0: jnp.where(b > 0, 0.5, 1.0), 4: jnp.where(b < m - 1, 0.5, 1.0)}
    one = jnp.full((ROWS, EZ), -1.0, f32)
    hz = {
        0: jnp.where(lane == 0, 0.0, -0.5).astype(f32),
        4: jnp.where(lane == EZ - 1, 0.0, -0.5).astype(f32),
    }

    def scale(i, j, k):
        side = hx.get(i, 1.0) * hy.get(j, 1.0)
        out = hz.get(k, one)
        return out * side.astype(f32) if i in hx or j in hy else out

    return scale


def pinned_line(u, lane):
    u[0] = jnp.where(lane == 0, 0.0, u[0])
    u[4] = jnp.where(lane == EZ - 1, 0.0, u[4])
    return u


def row_copies(src, dst, sem, first, count):
    return [
        pltpu.make_async_copy(
            src.at[r, pl.ds(first, count), 0, :], dst.at[pl.ds(first, count), r, :], sem.at[r]
        )
        for r in range(ROWS)
    ]


def opening_kernel(vel, conv, u8, cbuf, xa, xb, sem):
    a, b, n, m, ea, eb, ia, ja, sx, sy = place()
    copies = row_copies(vel, u8, sem.at[0], 0, PTS)
    faces = row_copies(conv, cbuf, sem.at[1], 0, 25) + row_copies(conv, cbuf, sem.at[2], 100, 25)
    inner = row_copies(conv, cbuf, sem.at[3], 25, 75)
    for c in copies + faces + inner:
        c.start()
    lane, odd_row = lane_index(), row_index() % 2 == 1
    scale = face_scale(lane, a, b, n, m)
    for c in copies + faces:
        c.wait()
    for i in (0, 4):
        gs, gt = {}, {}
        for k in range(NP):
            line = line_derivative([u8[pt(i, j, k), 0:ROWS] for j in range(NP)])
            for j in range(NP):
                gs[j, k] = line[j]
        for j in range(NP):
            line = line_derivative(pinned_line([u8[pt(i, j, k), 0:ROWS] for k in range(NP)], lane))
            for k in range(NP):
                gt[j, k] = line[k]
        for j in range(NP):
            w, cc = [], []
            for k in range(NP):
                c = cbuf[pt(i, j, k), 0:ROWS] * scale(i, j, k)
                ends = end_derivatives([u8[pt(q, j, k), 0:ROWS] for q in range(NP)])
                w.append(
                    widen(c[0:2], odd_row) * ends[i // 4]
                    + widen(c[2:4], odd_row) * gs[j, k]
                    + widen(c[4:6], odd_row) * gt[j, k]
                )
                cc.append(c)
            z_pair(w)
            c1 = [c[2:4] for c in cc]
            z_pair(c1)
            for k in range(NP):
                r = (j * NP + k) * 10
                if i == 0:
                    xa[r : r + 6], xa[r + 6 : r + 8], xa[r + 8 : r + 10] = w[k], c1[k], cc[k][4:6]
                else:
                    for lo, hi, new in ((0, 6, w[k]), (6, 8, c1[k]), (8, 10, cc[k][4:6])):
                        old = xa[r + lo : r + hi]
                        xa[r + lo : r + hi] = jnp.where(ea, new, old)
                        xb[r + lo : r + hi] = jnp.where(ea, old, new) * sx
    for c in inner:
        c.wait()


def coefficients(u8, cbuf, c0, c1, c2, w):
    a, b, n, m, ea, eb, ia, ja, sx, sy = place()
    lane, odd_row = lane_index(), row_index() % 2 == 1
    scale = face_scale(lane, a, b, n, m)
    for i in range(NP):
        for j in range(NP):
            for k in range(NP):
                p = pt(i, j, k)
                cc = cbuf[p, 0:ROWS] * scale(i, j, k)
                c0[p] = widen(cc[0:2], odd_row)
                c1[p] = widen(cc[2:4], odd_row)
                c2[p] = widen(cc[4:6], odd_row)
    for j in range(NP):
        for k in range(NP):
            g = line_derivative([u8[pt(i, j, k), 0:ROWS] for i in range(NP)])
            for i in range(NP):
                w[pt(i, j, k)] = c0[pt(i, j, k)] * g[i]
    for i in range(NP):
        for k in range(NP):
            g = line_derivative([u8[pt(i, j, k), 0:ROWS] for j in range(NP)])
            for j in range(NP):
                w[pt(i, j, k)] += c1[pt(i, j, k)] * g[j]
    for i in range(NP):
        for j in range(NP):
            g = line_derivative(pinned_line([u8[pt(i, j, k), 0:ROWS] for k in range(NP)], lane))
            line = [w[pt(i, j, k)] + c2[pt(i, j, k)] * g[k] for k in range(NP)]
            z_pair(line)
            for k in range(NP):
                w[pt(i, j, k)] = line[k]
            z_sum(c0, i * NP + j)
            z_sum(c1, i * NP + j)


def query_kernel(u8, cbuf, donor, coords, dest, target, table, c0, c1, c2, w):
    make_table(u8, donor, coords, dest, target, table)
    coefficients(u8, cbuf, c0, c1, c2, w)


def second_kernel(w, c0, c2, xa, xb, ya, yb):
    a, b, n, m, ea, eb, ia, ja, sx, sy = place()

    def edge(j_even, k, lo, hi, low_side):
        def at(j):
            r = (j * NP + k) * 10
            from_a, from_b = xa[r + lo : r + hi], xb[r + lo : r + hi]
            return jnp.where(ea, from_b, from_a) if low_side else jnp.where(ea, from_a, from_b)

        return jnp.where(j_even, at(4), at(0))

    for dst, jf, j_even, scale in ((ya, ja, eb, None), (yb, 4 - ja, jnp.logical_not(eb), sy)):
        put = (lambda x: x) if scale is None else (lambda x: x * scale)
        for i in range(NP):
            for k in range(NP):
                p = i * 25 + jf * NP + k
                r = (i * NP + k) * 10
                face = w[p]
                if i in (0, 4):
                    face = face + edge(j_even, k, 0, 6, i == 0)
                dst[r : r + 6] = put(face)
                dst[r + 6 : r + 8] = put(c0[p, 0:2])
                dst[r + 8 : r + 10] = put(c2[p, 0:2])
        for k in range(NP):
            for s, low_side in ((0, True), (1, False)):
                r = 250 + (s * NP + k) * 2
                dst[r : r + 2] = put(edge(j_even, k, 8, 10, low_side))


def make_table(u8, donor, coords, dest, target, table):
    queries = donor.shape[1]
    devices = table.shape[0]
    n, m = lax.axis_size("gx"), lax.axis_size("gy")
    lane_elem = donor[...] & (EZ - 1)
    hot = (
        lax.broadcasted_iota(jnp.int32, (EZ, queries), 0) == jnp.broadcast_to(lane_elem, (EZ, queries))
    ).astype(f32)
    grid = jnp.dot(
        u8[...].reshape(PTS * 8, EZ),
        hot,
        precision=lax.Precision.HIGHEST,
        preferred_element_type=f32,
    ).reshape(PTS, 8, queries)
    basis = []
    for d in range(3):
        x = coords[d : d + 1]
        line = []
        for i in range(NP):
            v = jnp.ones_like(x)
            for j in range(NP):
                if j != i:
                    v = v * ((x - NODES[j]) * (1.0 / (NODES[i] - NODES[j])))
            line.append(v)
        basis.append(line)
    total = jnp.zeros((8, queries), f32)
    for i in range(NP):
        for j in range(NP):
            part = grid[pt(i, j, 0)] * basis[2][0]
            for k in range(1, NP):
                part = part + grid[pt(i, j, k)] * basis[2][k]
            total = total + part * (basis[0][i] * basis[1][j])
    low = donor[...] < EZ
    rows = [jnp.where(low, total[2 * c : 2 * c + 1], total[2 * c + 1 : 2 * c + 2]) for c in range(3)]
    rows.append((target[...] + 1).astype(f32))
    row = lax.broadcasted_iota(jnp.int32, (8, queries), 0)
    packed = jnp.zeros((8, queries), f32)
    for r, x in enumerate(rows):
        packed = jnp.where(row == r, jnp.broadcast_to(x, (8, queries)), packed)
    goes = (
        lax.broadcasted_iota(jnp.int32, (devices, queries), 0)
        == jnp.broadcast_to(dest[...], (devices, queries))
    ).astype(f32)
    mine = lax.dot_general(
        packed,
        goes,
        (((1,), (1,)), ((), ())),
        precision=lax.Precision.HIGHEST,
        preferred_element_type=f32,
    )
    device = lax.broadcasted_iota(jnp.int32, (8, devices), 1)
    da, db = device // m, device % m

    def partner(x, pos, last, stride, first):
        even = pos % 2 == 0
        ahead, behind = pltpu.roll(x, devices - stride, 1), pltpu.roll(x, stride, 1)
        if first:
            return jnp.where(even, ahead, behind)
        return jnp.where((pos == 0) | (pos == last), 0.0, jnp.where(even, behind, ahead))

    x_a, x_b = partner(mine, da, n - 1, m, True), partner(mine, da, n - 1, m, False)
    slots = [mine, x_a, x_b]
    for first in (True, False):
        slots += [partner(s, db, m - 1, 1, first) for s in (mine, x_a, x_b)]
    slots.append(jnp.zeros((128 - SLOT * 9, devices), f32))
    table[...] = jnp.concatenate(slots, axis=0).T


def third_kernel(w_in, c0_in, c1_in, c2, xa, xb, ya, yb, table, v, c0, c1, z, oxa, oxb, oya, oyb, e):
    a, b, n, m, ea, eb, ia, ja, sx, sy = place()
    del w_in, c0_in, c1_in
    lane, row = lane_index(), row_index()
    odd_row = row % 2 == 1
    got = table[...].T
    base = (row % 2) * 50 + 1
    slope = [
        jnp.where(lane < EZ // 2, float(D[k, 0]), float(D[k, 4])).astype(f32) for k in range(NP)
    ]

    def values(slot, points):
        r = slot * SLOT
        mine = jnp.where(row < 2, got[r : r + 1], jnp.where(row < 4, got[r + 1 : r + 2], got[r + 2 : r + 3]))
        key = got[r + 3 : r + 4] - base.astype(f32)
        for where, ij in points:
            ends = []
            for side in range(2):
                hit = key == jnp.asarray(side * 25 + ij).astype(f32)
                ends.append(jnp.sum(jnp.where(hit, mine, 0.0), axis=1, keepdims=True))
            z[where] = jnp.where(lane == 0, ends[0], jnp.where(lane == EZ - 1, ends[1], 0.0))

    ib, jb = 4 - ia, 4 - ja
    values(0, [(ij, ij) for ij in range(25)])
    values(1, [(25 + j, ib * NP + j) for j in range(NP)])
    values(2, [(30 + j, ia * NP + j) for j in range(NP)])
    values(3, [(35 + i, i * NP + jb) for i in range(NP)])
    values(6, [(40 + i, i * NP + ja) for i in range(NP)])
    values(4, [(45, ib * NP + jb)])
    values(5, [(46, ia * NP + jb)])
    values(7, [(47, ib * NP + ja)])
    values(8, [(48, ia * NP + ja)])

    for ij in range(25):
        zz = z[ij]
        for k in range(NP):
            p = ij * NP + k
            e[p] = c2[p] * (zz * slope[k])
    for src, face, z0 in ((xa, ia, 25), (xb, ib, 30)):
        for j in range(NP):
            zz = z[z0 + j]
            for k in range(NP):
                r, p = (j * NP + k) * 10, face * 25 + j * NP + k
                v[p] += src[r : r + 6]
                c1[p] += widen(src[r + 6 : r + 8], odd_row)
                e[p] += widen(src[r + 8 : r + 10], odd_row) * (zz * slope[k])
    for src, face, z0, zd in ((ya, ja, 35, 45), (yb, jb, 40, 47)):
        for i in range(NP):
            zz = z[z0 + i]
            for k in range(NP):
                r, p = (i * NP + k) * 10, i * 25 + face * NP + k
                v[p] += src[r : r + 6]
                c0[p] += widen(src[r + 6 : r + 8], odd_row)
                add = widen(src[r + 8 : r + 10], odd_row) * (zz * slope[k])
                if i in (0, 4):
                    r = 250 + ((i // 4) * NP + k) * 2
                    through_a = ea if i == 4 else jnp.logical_not(ea)
                    zfar = jnp.where(through_a, z[zd], z[zd + 1])
                    add = add + widen(src[r : r + 2], odd_row) * (zfar * slope[k])
                e[p] += add
    for ij in range(25):
        line = [e[ij * NP + k] for k in range(NP)]
        z_pair(line)
        for k in range(NP):
            v[ij * NP + k] += line[k]
    second_messages(v, c1, oya, oyb)
    first_messages(v, c0, oxa, oxb)


def second_messages(v, c1, oya, oyb):
    a, b, n, m, ea, eb, ia, ja, sx, sy = place()
    for i in range(NP):
        for k in range(NP):
            low, high = end_derivatives([v[pt(i, j, k)] for j in range(NP)])
            low, high = low * c1[pt(i, 0, k)], high * c1[pt(i, 4, k)]
            r = (i * NP + k) * 6
            oya[r : r + 6] = jnp.where(eb, high, low)
            oyb[r : r + 6] = jnp.where(eb, low, high) * sy


def first_messages(v, c0, oxa, oxb):
    a, b, n, m, ea, eb, ia, ja, sx, sy = place()
    for j in range(NP):
        for k in range(NP):
            low, high = end_derivatives([v[pt(i, j, k)] for i in range(NP)])
            low, high = low * c0[pt(0, j, k)], high * c0[pt(4, j, k)]
            r = (j * NP + k) * 6
            oxa[r : r + 6] = jnp.where(ea, high, low)
            oxb[r : r + 6] = jnp.where(ea, low, high) * sx


def take_messages(v, xa, xb, ya, yb):
    a, b, n, m, ea, eb, ia, ja, sx, sy = place()
    for src, face in ((xa, ia), (xb, 4 - ia)):
        for jk in range(25):
            v[face * 25 + jk] += src[jk * 6 : jk * 6 + 6]
    for src, face in ((ya, ja), (yb, 4 - ja)):
        for i in range(NP):
            for k in range(NP):
                r = (i * NP + k) * 6
                v[i * 25 + face * NP + k] += src[r : r + 6]


def send_kernel(w_in, c0, c1, ya, yb, xb, xa, v, oxa, oxb, oya, oyb):
    del w_in
    take_messages(v, xa, xb, ya, yb)
    second_messages(v, c1, oya, oyb)
    first_messages(v, c0, oxa, oxb)


def sum_third(c2, xa, xb, ya, yb):
    a, b, n, m, ea, eb, ia, ja, sx, sy = place()
    odd_row = row_index() % 2 == 1
    for src, face in ((xa, ia), (xb, 4 - ia)):
        for jk in range(25):
            c2[face * 25 + jk] += widen(src[jk * 10 + 8 : jk * 10 + 10], odd_row)
    for src, face in ((ya, ja), (yb, 4 - ja)):
        for i in range(NP):
            for k in range(NP):
                r = (i * NP + k) * 10 + 8
                extra = src[r : r + 2]
                if i in (0, 4):
                    far = 250 + ((i // 4) * NP + k) * 2
                    extra = extra + src[far : far + 2]
                c2[i * 25 + face * NP + k] += widen(extra, odd_row)


def local_first_kernel(coef, v, c0, c1, c2_in, u8, z, xa, xb, ya, yb, acc, w, c2):
    del c2_in
    sum_third(c2, xa, xb, ya, yb)
    lane = lane_index()
    for ij in range(25):
        for k in range(NP):
            p = ij * NP + k
            u = u8[p, 0:ROWS]
            if k == 0:
                u = jnp.where(lane == 0, z[ij], u)
            if k == 4:
                u = jnp.where(lane == EZ - 1, z[ij], u)
            acc[p] = u + v[p] * coef
    apply(v, c0, c1, c2, w)


def local_kernel(coef, v, c0, c1, c2, acc_in, acc, w):
    del acc_in
    for p in range(PTS):
        acc[p] += v[p] * coef
    apply(v, c0, c1, c2, w)


def apply(v, c0, c1, c2, w):
    for j in range(NP):
        for k in range(NP):
            u = [v[pt(i, j, k)] for i in range(NP)]
            g = line_derivative(u)
            for i in range(NP):
                w[pt(i, j, k)] = c0[pt(i, j, k)] * g[i]
    for i in range(NP):
        for k in range(NP):
            g = line_derivative([v[pt(i, j, k)] for j in range(NP)])
            for j in range(NP):
                w[pt(i, j, k)] += c1[pt(i, j, k)] * g[j]
    for i in range(NP):
        for j in range(NP):
            g = line_derivative([v[pt(i, j, k)] for k in range(NP)])
            t = [c2[pt(i, j, k)] * g[k] for k in range(NP)]
            z_pair(t)
            for k in range(NP):
                w[pt(i, j, k)] += t[k]


def last_kernel(coef, w_in, acc, ya, yb, xb, xa, v, out, obuf, sem):
    del w_in
    take_messages(v, xa, xb, ya, yb)
    started = []
    for i in range(NP):
        for p in range(i * 25, i * 25 + 25):
            obuf[p, 0:ROWS] = acc[p] + v[p] * coef
        for r in range(ROWS):
            rows = pl.ds(i * 25, 25)
            c = pltpu.make_async_copy(obuf.at[rows, r, :], out.at[r, rows, 0, :], sem.at[i, r])
            c.start()
            started.append(c)
    for c in started:
        c.wait()


FIELD = (PTS, ROWS, EZ)


RAW = (ROWS, PTS, 1, EZ)


def call(kernel, outs, args, aliases=None, scratch=(), flops=0, limit=24):
    moved = sum(4 * math.prod(x.shape) for x in args) + sum(4 * math.prod(s) for s in outs)
    spec = lambda shape: pl.BlockSpec(memory_space=pl.ANY if shape == RAW else pltpu.VMEM)
    return pl.pallas_call(
        kernel,
        out_shape=[jax.ShapeDtypeStruct(s, f32) for s in outs],
        in_specs=[spec(x.shape) for x in args],
        out_specs=[spec(s) for s in outs],
        input_output_aliases=aliases or {},
        scratch_shapes=list(scratch),
        compiler_params=pltpu.CompilerParams(vmem_limit_bytes=limit * 1024 * 1024),
        cost_estimate=pl.CostEstimate(flops=flops, bytes_accessed=moved, transcendentals=0),
    )(*args)


def pairs(size, offset):
    route = []
    for low in range(offset, size, 2):
        high = (low + 1) % size
        route += [(low, high), (high, low)]
    return route


def swap(x, axis, offset):
    return lax.ppermute(x, axis, pairs(lax.axis_size(axis), offset))


def swap_all(xa, xb, ya, yb):
    return swap(xa, "gx", 0), swap(xb, "gx", 1), swap(ya, "gy", 0), swap(yb, "gy", 1)


def body(velocity, convecting, donor_element, coords, dest_rank, target):
    devices = lax.axis_size("gx") * lax.axis_size("gy")
    queries = dest_rank.shape[0]
    vel, conv = velocity.reshape(RAW), convecting.reshape(RAW)
    vel, conv = (pltpu.with_memory_space_constraint(x, pltpu.HBM) for x in (vel, conv))
    whole = pltpu.VMEM((PTS, 8, EZ), f32)
    u8, cbuf, xa, xb = call(
        opening_kernel,
        [(PTS, 8, EZ)] * 2 + [(250, EZ)] * 2,
        [vel, conv],
        scratch=[pltpu.SemaphoreType.DMA((4, ROWS))],
        limit=24,
    )
    fxa, fxb = swap(xa, "gx", 0), swap(xb, "gx", 1)
    table, c0, c1, c2, w = call(
        query_kernel,
        [(devices, 128)] + [FIELD] * 4,
        [
            u8,
            cbuf,
            donor_element.reshape(1, queries),
            coords,
            dest_rank.reshape(1, queries),
            target.reshape(1, queries),
        ],
    )
    ya, yb = call(second_kernel, [(270, EZ)] * 2, [w, c0, c2, fxa, fxb])
    table, ya, yb = lax.optimization_barrier((table, ya, yb))
    fya, fyb = swap(ya, "gy", 0), swap(yb, "gy", 1)
    table = lax.all_to_all(table.reshape(devices, 1, 128), ("gx", "gy"), 0, 0).reshape(devices, 128)
    v, c0, c1, z, xa, xb, ya, yb = call(
        third_kernel,
        [FIELD] * 3 + [(49, ROWS, EZ)] + [(150, EZ)] * 4,
        [w, c0, c1, c2, fxa, fxb, fya, fyb, table],
        aliases={0: 0, 1: 1, 2: 2},
        scratch=[pltpu.VMEM(FIELD, f32)],
    )
    coef = 1.0
    for stage in range(1, 4):
        coef = coef * time_step / stage
        xa, xb = swap(xa, "gx", 0), swap(xb, "gx", 1)
        ya, yb = swap(ya, "gy", 0), swap(yb, "gy", 1)
        got = [ya, yb, xb, xa]
        if stage == 1:
            acc, w, c2 = call(
                functools.partial(local_first_kernel, coef),
                [FIELD] * 3,
                [v, c0, c1, c2, u8, z, fxa, fxb, fya, fyb],
                aliases={3: 2},
                flops=10**7,
            )
        else:
            acc, w = call(
                functools.partial(local_kernel, coef),
                [FIELD] * 2,
                [v, c0, c1, c2, acc],
                aliases={4: 0},
                flops=10**7,
            )
        if stage < 3:
            v, xa, xb, ya, yb = call(
                send_kernel, [FIELD] + [(150, EZ)] * 4, [w, c0, c1, *got], aliases={0: 0}
            )
    coef = coef * time_step / 4
    _, out = call(
        functools.partial(last_kernel, coef),
        [FIELD, RAW],
        [w, acc, *got],
        aliases={0: 0},
        scratch=[whole, pltpu.SemaphoreType.DMA((NP, ROWS))],
    )
    return out.reshape(velocity.shape)


def solution(mesh):
    field = P(None, None, None, None, None, "gx", "gy", None)
    return jax.shard_map(
        body,
        mesh=mesh,
        in_specs=(field, field, P(("gx", "gy")), P(None, ("gx", "gy")), P(("gx", "gy")), P(("gx", "gy"))),
        out_specs=field,
        check_vma=False,
    )
```

```python
import functools
import math

import jax
import jax.numpy as jnp
import numpy as np
from jax import lax
from jax.experimental import pallas as pl
from jax.experimental.pallas import tpu as pltpu
from jax.sharding import PartitionSpec as P

time_step = 0.04
NP = 5
PTS = NP * NP * NP
ROWS = 6
EZ = 256
SLOT = 8
f32 = jnp.float32


def gll_tables():
    root_value = math.sqrt(3.0 / 7.0)
    nodes = [-1.0, -root_value, 0.0, root_value, 1.0]
    bary = []
    for i in range(NP):
        product = 1.0
        for j in range(NP):
            if j != i:
                product = product * (nodes[i] - nodes[j])
        bary.append(1.0 / product)
    table = np.zeros((NP, NP))
    for a in range(NP):
        for i in range(NP):
            if a != i:
                table[a, i] = bary[i] / bary[a] / (nodes[a] - nodes[i])
        table[a, a] = -np.sum(table[a])
    return nodes, table


NODES, D = gll_tables()


def pt(i, j, k):
    return (i * NP + j) * NP + k


def line_derivative(u):
    d0, d1 = u[0] - u[4], u[1] - u[3]
    s0, s1 = u[0] + u[4], u[1] + u[3]
    out = [None] * NP
    out[2] = d0 * float(D[2, 0]) + d1 * float(D[2, 1])
    for a in (0, 1):
        odd = d0 * float((D[a, 0] - D[a, 4]) / 2) + d1 * float((D[a, 1] - D[a, 3]) / 2)
        even = (
            s0 * float((D[a, 0] + D[a, 4]) / 2)
            + s1 * float((D[a, 1] + D[a, 3]) / 2)
            + u[2] * float(D[a, 2])
        )
        out[a] = odd + even
        out[4 - a] = odd - even
    return out


def end_derivatives(u):
    d0, d1 = u[0] - u[4], u[1] - u[3]
    s0, s1 = u[0] + u[4], u[1] + u[3]
    odd = d0 * float((D[0, 0] - D[0, 4]) / 2) + d1 * float((D[0, 1] - D[0, 3]) / 2)
    even = (
        s0 * float((D[0, 0] + D[0, 4]) / 2)
        + s1 * float((D[0, 1] + D[0, 3]) / 2)
        + u[2] * float(D[0, 2])
    )
    return odd + even, odd - even


def lane_index():
    return lax.broadcasted_iota(jnp.int32, (ROWS, EZ), 1)


def row_index():
    return lax.broadcasted_iota(jnp.int32, (ROWS, EZ), 0)


def place():
    a, b = lax.axis_index("gx"), lax.axis_index("gy")
    n, m = lax.axis_size("gx"), lax.axis_size("gy")
    ea, eb = a % 2 == 0, b % 2 == 0
    ia, ja = jnp.where(ea, 4, 0), jnp.where(eb, 4, 0)
    sx = jnp.where((a == 0) | (a == n - 1), 0.0, 1.0).astype(f32)
    sy = jnp.where((b == 0) | (b == m - 1), 0.0, 1.0).astype(f32)
    return a, b, n, m, ea, eb, ia, ja, sx, sy


def widen(two, odd_row):
    return jnp.where(odd_row, two[1:2], two[0:1])


def z_pair(line):
    line[0], line[4] = line[0] + pltpu.roll(line[4], 1, 1), line[4] + pltpu.roll(line[0], EZ - 1, 1)


def z_sum(ref, ij):
    line = [ref[ij * NP + k] for k in range(NP)]
    z_pair(line)
    ref[ij * NP], ref[ij * NP + 4] = line[0], line[4]


def face_scale(lane, a, b, n, m):
    hx = {0: jnp.where(a > 0, 0.5, 1.0), 4: jnp.where(a < n - 1, 0.5, 1.0)}
    hy = {0: jnp.where(b > 0, 0.5, 1.0), 4: jnp.where(b < m - 1, 0.5, 1.0)}
    one = jnp.full((ROWS, EZ), -1.0, f32)
    hz = {
        0: jnp.where(lane == 0, 0.0, -0.5).astype(f32),
        4: jnp.where(lane == EZ - 1, 0.0, -0.5).astype(f32),
    }

    def scale(i, j, k):
        side = hx.get(i, 1.0) * hy.get(j, 1.0)
        out = hz.get(k, one)
        return out * side.astype(f32) if i in hx or j in hy else out

    return scale


def pinned_line(u, lane):
    u[0] = jnp.where(lane == 0, 0.0, u[0])
    u[4] = jnp.where(lane == EZ - 1, 0.0, u[4])
    return u


def row_copies(src, dst, sem, first, count):
    return [
        pltpu.make_async_copy(
            src.at[r, pl.ds(first, count), 0, :], dst.at[pl.ds(first, count), r, :], sem.at[r]
        )
        for r in range(ROWS)
    ]


def opening_kernel(vel, conv, u8, cbuf, xa, xb, sem):
    a, b, n, m, ea, eb, ia, ja, sx, sy = place()
    copies = row_copies(vel, u8, sem.at[0], 0, PTS)
    faces = row_copies(conv, cbuf, sem.at[1], 0, 25) + row_copies(conv, cbuf, sem.at[2], 100, 25)
    inner = row_copies(conv, cbuf, sem.at[3], 25, 75)
    for c in copies + faces + inner:
        c.start()
    lane, odd_row = lane_index(), row_index() % 2 == 1
    scale = face_scale(lane, a, b, n, m)
    for c in copies + faces:
        c.wait()
    for i in (0, 4):
        gs, gt = {}, {}
        for k in range(NP):
            line = line_derivative([u8[pt(i, j, k), 0:ROWS] for j in range(NP)])
            for j in range(NP):
                gs[j, k] = line[j]
        for j in range(NP):
            line = line_derivative(pinned_line([u8[pt(i, j, k), 0:ROWS] for k in range(NP)], lane))
            for k in range(NP):
                gt[j, k] = line[k]
        for j in range(NP):
            w, cc = [], []
            for k in range(NP):
                c = cbuf[pt(i, j, k), 0:ROWS] * scale(i, j, k)
                ends = end_derivatives([u8[pt(q, j, k), 0:ROWS] for q in range(NP)])
                w.append(
                    widen(c[0:2], odd_row) * ends[i // 4]
                    + widen(c[2:4], odd_row) * gs[j, k]
                    + widen(c[4:6], odd_row) * gt[j, k]
                )
                cc.append(c)
            z_pair(w)
            c1 = [c[2:4] for c in cc]
            z_pair(c1)
            for k in range(NP):
                r = (j * NP + k) * 10
                if i == 0:
                    xa[r : r + 6], xa[r + 6 : r + 8], xa[r + 8 : r + 10] = w[k], c1[k], cc[k][4:6]
                else:
                    for lo, hi, new in ((0, 6, w[k]), (6, 8, c1[k]), (8, 10, cc[k][4:6])):
                        old = xa[r + lo : r + hi]
                        xa[r + lo : r + hi] = jnp.where(ea, new, old)
                        xb[r + lo : r + hi] = jnp.where(ea, old, new) * sx
    for c in inner:
        c.wait()


def coefficients(u8, cbuf, c0, c1, c2, w):
    a, b, n, m, ea, eb, ia, ja, sx, sy = place()
    lane, odd_row = lane_index(), row_index() % 2 == 1
    scale = face_scale(lane, a, b, n, m)
    for i in range(NP):
        for j in range(NP):
            for k in range(NP):
                p = pt(i, j, k)
                cc = cbuf[p, 0:ROWS] * scale(i, j, k)
                c0[p] = widen(cc[0:2], odd_row)
                c1[p] = widen(cc[2:4], odd_row)
                c2[p] = widen(cc[4:6], odd_row)
    for j in range(NP):
        for k in range(NP):
            g = line_derivative([u8[pt(i, j, k), 0:ROWS] for i in range(NP)])
            for i in range(NP):
                w[pt(i, j, k)] = c0[pt(i, j, k)] * g[i]
    for i in range(NP):
        for k in range(NP):
            g = line_derivative([u8[pt(i, j, k), 0:ROWS] for j in range(NP)])
            for j in range(NP):
                w[pt(i, j, k)] += c1[pt(i, j, k)] * g[j]
    for i in range(NP):
        for j in range(NP):
            g = line_derivative(pinned_line([u8[pt(i, j, k), 0:ROWS] for k in range(NP)], lane))
            line = [w[pt(i, j, k)] + c2[pt(i, j, k)] * g[k] for k in range(NP)]
            z_pair(line)
            for k in range(NP):
                w[pt(i, j, k)] = line[k]
            z_sum(c0, i * NP + j)
            z_sum(c1, i * NP + j)


def query_kernel(u8, cbuf, donor, coords, dest, target, table, c0, c1, c2, w):
    make_table(u8, donor, coords, dest, target, table)
    coefficients(u8, cbuf, c0, c1, c2, w)


def second_kernel(w, c0, c2, xa, xb, ya, yb):
    a, b, n, m, ea, eb, ia, ja, sx, sy = place()

    def edge(j_even, k, lo, hi, low_side):
        def at(j):
            r = (j * NP + k) * 10
            from_a, from_b = xa[r + lo : r + hi], xb[r + lo : r + hi]
            return jnp.where(ea, from_b, from_a) if low_side else jnp.where(ea, from_a, from_b)

        return jnp.where(j_even, at(4), at(0))

    for dst, jf, j_even, scale in ((ya, ja, eb, None), (yb, 4 - ja, jnp.logical_not(eb), sy)):
        put = (lambda x: x) if scale is None else (lambda x: x * scale)
        for i in range(NP):
            for k in range(NP):
                p = i * 25 + jf * NP + k
                r = (i * NP + k) * 10
                face = w[p]
                if i in (0, 4):
                    face = face + edge(j_even, k, 0, 6, i == 0)
                dst[r : r + 6] = put(face)
                dst[r + 6 : r + 8] = put(c0[p, 0:2])
                dst[r + 8 : r + 10] = put(c2[p, 0:2])
        for k in range(NP):
            for s, low_side in ((0, True), (1, False)):
                r = 250 + (s * NP + k) * 2
                dst[r : r + 2] = put(edge(j_even, k, 8, 10, low_side))


def make_table(u8, donor, coords, dest, target, table):
    queries = donor.shape[1]
    devices = table.shape[0]
    n, m = lax.axis_size("gx"), lax.axis_size("gy")
    lane_elem = donor[...] & (EZ - 1)
    hot = (
        lax.broadcasted_iota(jnp.int32, (EZ, queries), 0) == jnp.broadcast_to(lane_elem, (EZ, queries))
    ).astype(f32)
    grid = jnp.dot(
        u8[...].reshape(PTS * 8, EZ),
        hot,
        precision=lax.Precision.HIGHEST,
        preferred_element_type=f32,
    ).reshape(PTS, 8, queries)
    basis = []
    for d in range(3):
        x = coords[d : d + 1]
        line = []
        for i in range(NP):
            v = jnp.ones_like(x)
            for j in range(NP):
                if j != i:
                    v = v * ((x - NODES[j]) * (1.0 / (NODES[i] - NODES[j])))
            line.append(v)
        basis.append(line)
    total = jnp.zeros((8, queries), f32)
    for i in range(NP):
        for j in range(NP):
            part = grid[pt(i, j, 0)] * basis[2][0]
            for k in range(1, NP):
                part = part + grid[pt(i, j, k)] * basis[2][k]
            total = total + part * (basis[0][i] * basis[1][j])
    low = donor[...] < EZ
    rows = [jnp.where(low, total[2 * c : 2 * c + 1], total[2 * c + 1 : 2 * c + 2]) for c in range(3)]
    rows.append((target[...] + 1).astype(f32))
    row = lax.broadcasted_iota(jnp.int32, (8, queries), 0)
    packed = jnp.zeros((8, queries), f32)
    for r, x in enumerate(rows):
        packed = jnp.where(row == r, jnp.broadcast_to(x, (8, queries)), packed)
    goes = (
        lax.broadcasted_iota(jnp.int32, (devices, queries), 0)
        == jnp.broadcast_to(dest[...], (devices, queries))
    ).astype(f32)
    mine = lax.dot_general(
        packed,
        goes,
        (((1,), (1,)), ((), ())),
        precision=lax.Precision.HIGHEST,
        preferred_element_type=f32,
    )
    device = lax.broadcasted_iota(jnp.int32, (8, devices), 1)
    da, db = device // m, device % m

    def partner(x, pos, last, stride, first):
        even = pos % 2 == 0
        ahead, behind = pltpu.roll(x, devices - stride, 1), pltpu.roll(x, stride, 1)
        if first:
            return jnp.where(even, ahead, behind)
        return jnp.where((pos == 0) | (pos == last), 0.0, jnp.where(even, behind, ahead))

    x_a, x_b = partner(mine, da, n - 1, m, True), partner(mine, da, n - 1, m, False)
    slots = [mine, x_a, x_b]
    for first in (True, False):
        slots += [partner(s, db, m - 1, 1, first) for s in (mine, x_a, x_b)]
    slots.append(jnp.zeros((128 - SLOT * 9, devices), f32))
    table[...] = jnp.concatenate(slots, axis=0).T


def third_kernel(w_in, c0_in, c1_in, c2, xa, xb, ya, yb, table, v, c0, c1, z, oxa, oxb, oya, oyb, e):
    a, b, n, m, ea, eb, ia, ja, sx, sy = place()
    del w_in, c0_in, c1_in
    lane, row = lane_index(), row_index()
    odd_row = row % 2 == 1
    got = table[...].T
    base = (row % 2) * 50 + 1
    slope = [
        jnp.where(lane < EZ // 2, float(D[k, 0]), float(D[k, 4])).astype(f32) for k in range(NP)
    ]

    def values(slot, points):
        r = slot * SLOT
        mine = jnp.where(row < 2, got[r : r + 1], jnp.where(row < 4, got[r + 1 : r + 2], got[r + 2 : r + 3]))
        key = got[r + 3 : r + 4] - base.astype(f32)
        for where, ij in points:
            ends = []
            for side in range(2):
                hit = key == jnp.asarray(side * 25 + ij).astype(f32)
                ends.append(jnp.sum(jnp.where(hit, mine, 0.0), axis=1, keepdims=True))
            z[where] = jnp.where(lane == 0, ends[0], jnp.where(lane == EZ - 1, ends[1], 0.0))

    ib, jb = 4 - ia, 4 - ja
    values(0, [(ij, ij) for ij in range(25)])
    values(1, [(25 + j, ib * NP + j) for j in range(NP)])
    values(2, [(30 + j, ia * NP + j) for j in range(NP)])
    values(3, [(35 + i, i * NP + jb) for i in range(NP)])
    values(6, [(40 + i, i * NP + ja) for i in range(NP)])
    values(4, [(45, ib * NP + jb)])
    values(5, [(46, ia * NP + jb)])
    values(7, [(47, ib * NP + ja)])
    values(8, [(48, ia * NP + ja)])

    for ij in range(25):
        zz = z[ij]
        for k in range(NP):
            p = ij * NP + k
            e[p] = c2[p] * (zz * slope[k])
    for src, face, z0 in ((xa, ia, 25), (xb, ib, 30)):
        for j in range(NP):
            zz = z[z0 + j]
            for k in range(NP):
                r, p = (j * NP + k) * 10, face * 25 + j * NP + k
                v[p] += src[r : r + 6]
                c1[p] += widen(src[r + 6 : r + 8], odd_row)
                e[p] += widen(src[r + 8 : r + 10], odd_row) * (zz * slope[k])
    for src, face, z0, zd in ((ya, ja, 35, 45), (yb, jb, 40, 47)):
        for i in range(NP):
            zz = z[z0 + i]
            for k in range(NP):
                r, p = (i * NP + k) * 10, i * 25 + face * NP + k
                v[p] += src[r : r + 6]
                c0[p] += widen(src[r + 6 : r + 8], odd_row)
                add = widen(src[r + 8 : r + 10], odd_row) * (zz * slope[k])
                if i in (0, 4):
                    r = 250 + ((i // 4) * NP + k) * 2
                    through_a = ea if i == 4 else jnp.logical_not(ea)
                    zfar = jnp.where(through_a, z[zd], z[zd + 1])
                    add = add + widen(src[r : r + 2], odd_row) * (zfar * slope[k])
                e[p] += add
    for ij in range(25):
        line = [e[ij * NP + k] for k in range(NP)]
        z_pair(line)
        for k in range(NP):
            v[ij * NP + k] += line[k]
    second_messages(v, c1, oya, oyb)
    first_messages(v, c0, oxa, oxb)


def second_messages(v, c1, oya, oyb):
    a, b, n, m, ea, eb, ia, ja, sx, sy = place()
    for i in range(NP):
        for k in range(NP):
            low, high = end_derivatives([v[pt(i, j, k)] for j in range(NP)])
            low, high = low * c1[pt(i, 0, k)], high * c1[pt(i, 4, k)]
            r = (i * NP + k) * 6
            oya[r : r + 6] = jnp.where(eb, high, low)
            oyb[r : r + 6] = jnp.where(eb, low, high) * sy


def first_messages(v, c0, oxa, oxb):
    a, b, n, m, ea, eb, ia, ja, sx, sy = place()
    for j in range(NP):
        for k in range(NP):
            low, high = end_derivatives([v[pt(i, j, k)] for i in range(NP)])
            low, high = low * c0[pt(0, j, k)], high * c0[pt(4, j, k)]
            r = (j * NP + k) * 6
            oxa[r : r + 6] = jnp.where(ea, high, low)
            oxb[r : r + 6] = jnp.where(ea, low, high) * sx


def take_messages(v, xa, xb, ya, yb):
    a, b, n, m, ea, eb, ia, ja, sx, sy = place()
    for src, face in ((xa, ia), (xb, 4 - ia)):
        for jk in range(25):
            v[face * 25 + jk] += src[jk * 6 : jk * 6 + 6]
    for src, face in ((ya, ja), (yb, 4 - ja)):
        for i in range(NP):
            for k in range(NP):
                r = (i * NP + k) * 6
                v[i * 25 + face * NP + k] += src[r : r + 6]


def send_kernel(w_in, c0, c1, ya, xb, yb, xa, v, oxa, oxb, oya, oyb):
    del w_in
    take_messages(v, xa, xb, ya, yb)
    second_messages(v, c1, oya, oyb)
    first_messages(v, c0, oxa, oxb)


def sum_third(c2, xa, xb, ya, yb):
    a, b, n, m, ea, eb, ia, ja, sx, sy = place()
    odd_row = row_index() % 2 == 1
    for src, face in ((xa, ia), (xb, 4 - ia)):
        for jk in range(25):
            c2[face * 25 + jk] += widen(src[jk * 10 + 8 : jk * 10 + 10], odd_row)
    for src, face in ((ya, ja), (yb, 4 - ja)):
        for i in range(NP):
            for k in range(NP):
                r = (i * NP + k) * 10 + 8
                extra = src[r : r + 2]
                if i in (0, 4):
                    far = 250 + ((i // 4) * NP + k) * 2
                    extra = extra + src[far : far + 2]
                c2[i * 25 + face * NP + k] += widen(extra, odd_row)


def local_first_kernel(coef, v, c0, c1, c2_in, u8, z, xa, xb, ya, yb, acc, w, c2):
    del c2_in
    sum_third(c2, xa, xb, ya, yb)
    lane = lane_index()
    for ij in range(25):
        for k in range(NP):
            p = ij * NP + k
            u = u8[p, 0:ROWS]
            if k == 0:
                u = jnp.where(lane == 0, z[ij], u)
            if k == 4:
                u = jnp.where(lane == EZ - 1, z[ij], u)
            acc[p] = u + v[p] * coef
    apply(v, c0, c1, c2, w)


def local_kernel(coef, v, c0, c1, c2, acc_in, acc, w):
    del acc_in
    for p in range(PTS):
        acc[p] += v[p] * coef
    apply(v, c0, c1, c2, w)


def apply(v, c0, c1, c2, w):
    for j in range(NP):
        for k in range(NP):
            u = [v[pt(i, j, k)] for i in range(NP)]
            g = line_derivative(u)
            for i in range(NP):
                w[pt(i, j, k)] = c0[pt(i, j, k)] * g[i]
    for i in range(NP):
        for k in range(NP):
            g = line_derivative([v[pt(i, j, k)] for j in range(NP)])
            for j in range(NP):
                w[pt(i, j, k)] += c1[pt(i, j, k)] * g[j]
    for i in range(NP):
        for j in range(NP):
            g = line_derivative([v[pt(i, j, k)] for k in range(NP)])
            t = [c2[pt(i, j, k)] * g[k] for k in range(NP)]
            z_pair(t)
            for k in range(NP):
                w[pt(i, j, k)] += t[k]


def last_kernel(coef, w_in, acc, ya, xb, yb, xa, v, out, obuf, sem):
    del w_in
    take_messages(v, xa, xb, ya, yb)
    started = []
    for i in range(NP):
        for p in range(i * 25, i * 25 + 25):
            obuf[p, 0:ROWS] = acc[p] + v[p] * coef
        for r in range(ROWS):
            rows = pl.ds(i * 25, 25)
            c = pltpu.make_async_copy(obuf.at[rows, r, :], out.at[r, rows, 0, :], sem.at[i, r])
            c.start()
            started.append(c)
    for c in started:
        c.wait()


FIELD = (PTS, ROWS, EZ)


RAW = (ROWS, PTS, 1, EZ)


def call(kernel, outs, args, aliases=None, scratch=(), flops=0, limit=24):
    moved = sum(4 * math.prod(x.shape) for x in args) + sum(4 * math.prod(s) for s in outs)
    spec = lambda shape: pl.BlockSpec(memory_space=pl.ANY if shape == RAW else pltpu.VMEM)
    return pl.pallas_call(
        kernel,
        out_shape=[jax.ShapeDtypeStruct(s, f32) for s in outs],
        in_specs=[spec(x.shape) for x in args],
        out_specs=[spec(s) for s in outs],
        input_output_aliases=aliases or {},
        scratch_shapes=list(scratch),
        compiler_params=pltpu.CompilerParams(vmem_limit_bytes=limit * 1024 * 1024),
        cost_estimate=pl.CostEstimate(flops=flops, bytes_accessed=moved, transcendentals=0),
    )(*args)


def pairs(size, offset):
    route = []
    for low in range(offset, size, 2):
        high = (low + 1) % size
        route += [(low, high), (high, low)]
    return route


def swap(x, axis, offset):
    return lax.ppermute(x, axis, pairs(lax.axis_size(axis), offset))


def swap_all(xa, xb, ya, yb):
    return swap(xa, "gx", 0), swap(xb, "gx", 1), swap(ya, "gy", 0), swap(yb, "gy", 1)


def body(velocity, convecting, donor_element, coords, dest_rank, target):
    devices = lax.axis_size("gx") * lax.axis_size("gy")
    queries = dest_rank.shape[0]
    vel, conv = velocity.reshape(RAW), convecting.reshape(RAW)
    vel, conv = (pltpu.with_memory_space_constraint(x, pltpu.HBM) for x in (vel, conv))
    whole = pltpu.VMEM((PTS, 8, EZ), f32)
    u8, cbuf, xa, xb = call(
        opening_kernel,
        [(PTS, 8, EZ)] * 2 + [(250, EZ)] * 2,
        [vel, conv],
        scratch=[pltpu.SemaphoreType.DMA((4, ROWS))],
        limit=24,
    )
    fxa, fxb = swap(xa, "gx", 0), swap(xb, "gx", 1)
    table, c0, c1, c2, w = call(
        query_kernel,
        [(devices, 128)] + [FIELD] * 4,
        [
            u8,
            cbuf,
            donor_element.reshape(1, queries),
            coords,
            dest_rank.reshape(1, queries),
            target.reshape(1, queries),
        ],
    )
    ya, yb = call(second_kernel, [(270, EZ)] * 2, [w, c0, c2, fxa, fxb])
    table, ya, yb = lax.optimization_barrier((table, ya, yb))
    fya, fyb = swap(ya, "gy", 0), swap(yb, "gy", 1)
    table = lax.all_to_all(table.reshape(devices, 1, 128), ("gx", "gy"), 0, 0).reshape(devices, 128)
    v, c0, c1, z, xa, xb, ya, yb = call(
        third_kernel,
        [FIELD] * 3 + [(49, ROWS, EZ)] + [(150, EZ)] * 4,
        [w, c0, c1, c2, fxa, fxb, fya, fyb, table],
        aliases={0: 0, 1: 1, 2: 2},
        scratch=[pltpu.VMEM(FIELD, f32)],
    )
    coef = 1.0
    for stage in range(1, 4):
        coef = coef * time_step / stage
        xa, xb = swap(xa, "gx", 0), swap(xb, "gx", 1)
        ya, yb = swap(ya, "gy", 0), swap(yb, "gy", 1)
        got = [ya, xb, yb, xa]
        if stage == 1:
            acc, w, c2 = call(
                functools.partial(local_first_kernel, coef),
                [FIELD] * 3,
                [v, c0, c1, c2, u8, z, fxa, fxb, fya, fyb],
                aliases={3: 2},
                flops=10**7,
            )
        else:
            acc, w = call(
                functools.partial(local_kernel, coef),
                [FIELD] * 2,
                [v, c0, c1, c2, acc],
                aliases={4: 0},
                flops=10**7,
            )
        if stage < 3:
            v, xa, xb, ya, yb = call(
                send_kernel, [FIELD] + [(150, EZ)] * 4, [w, c0, c1, *got], aliases={0: 0}
            )
    coef = coef * time_step / 4
    _, out = call(
        functools.partial(last_kernel, coef),
        [FIELD, RAW],
        [w, acc, *got],
        aliases={0: 0},
        scratch=[whole, pltpu.SemaphoreType.DMA((NP, ROWS))],
    )
    return out.reshape(velocity.shape)


def solution(mesh):
    field = P(None, None, None, None, None, "gx", "gy", None)
    return jax.shard_map(
        body,
        mesh=mesh,
        in_specs=(field, field, P(("gx", "gy")), P(None, ("gx", "gy")), P(("gx", "gy")), P(("gx", "gy"))),
        out_specs=field,
        check_vma=False,
    )
```
